128 devices in a mesh: view: 4 (over y_lo, core), tile: 32 (over z, y_hi, x).
Axes of the slice: x: 4, y: 4 (y_hi: 2, y_lo: 2; y = y_hi * 2 + y_lo), z: 4, core: 2. Of those that a mesh axis runs over, the one named last changes fastest.
Arguments:
- source_features: bfloat16 [20, 32, 256, 128], P('view', None, 'tile'), may hold values from -6 to 6
- reference_features: bfloat16 [32, 32768], P(None, 'tile'), may hold values from -6 to 6
- interp: bfloat16 [20, 8, 4, 64, 64], P('view'), may hold values from -0.375 to 0.375
- source_tile: int32 [20, 8, 512, 4], P('view', None, 'tile'), may hold values from -1 to 1
- source_block: int32 [20, 8, 512, 4], P('view', None, 'tile'), may hold values from 0 to 15
- conv_weight: bfloat16 [3, 3, 3, 8, 32], replicated, may hold values from -0.21875 to 0.21875
- grad_regularized: bfloat16 [8, 8, 32768], P('view', None, 'tile'), may hold values from -6 to 6
Outputs:
- regularized: bfloat16 [8, 8, 32768], P('view', None, 'tile')
- grad_source: float32 [20, 32, 256, 128], P('view', None, 'tile')
The draws below stay inside these ranges and needn't reach their ends.
Inputs may be any that keep to these rules, and one draw needn't show every extreme that they name: source_tile is the offset of a source block's row tile from the tile of the output block it feeds. source_block is the block's index within that row tile.
All inputs are finite; a program needn't handle non-finite values.
Results may differ from the reference program's by a relative error of at most 0.0056.
Values may be sent and summed in bfloat16 or wider, within the bound.
No kernel may reach another device: no remote copies, remote signals or barrier semaphores. Data moves between devices by JAX's collectives and lax.ppermute only.
A program may use at most 128 MiB of HBM per device.

```python
import jax
import jax.numpy as jnp
from jax import lax

CH = 32
OUT_CH = 8
BLK = 64
TAPS = 4
ROWS_DEV = 4
COLS = 256
V = 20
D = 8
H = 128
NPIX = 32768
NB = 16
NBLK = 512
N_TILE = 32


def set_ends(array, rng, smallest, high):
    index_at = [jax.random.randint(jax.random.fold_in(rng, axis), (), 0, length) for axis, length in enumerate(array.shape)]
    widest = array.shape.index(max(array.shape))
    neighbour = index_at[:widest] + [(index_at[widest] + 1) % array.shape[widest]] + index_at[widest + 1:]
    return array.at[tuple(index_at)].set(smallest).at[tuple(neighbour)].set(high)


def level_of(key, shape, shards, least, high):
    gain = 1.0
    for position, blocks in shards:
        draws = jax.random.uniform(jax.random.fold_in(jax.random.fold_in(key, 6), position), (blocks,), jnp.float32, least / len(shards), high / len(shards))
        gain = gain * jnp.repeat(jnp.exp(draws), shape[position] // blocks).reshape((-1,) + (1,) * (len(shape) - 1 - position))
    return gain


def centred(own_key, shape, deviation, most, cuts=(), kind=jnp.bfloat16):
    drawn = jax.random.normal(own_key, shape, jnp.float32) * deviation
    if len(cuts) > 0:
        drawn = level_of(own_key, shape, cuts, -0.22, 0.18) * drawn
    return jnp.clip(drawn, min=-most, max=most).astype(kind)


def setup_inputs(seed: int = 0) -> dict:
    splits = jax.random.split(jax.random.key(seed), 8)
    return {
        "source_features": centred(splits[0], (V, CH, COLS, H), 1.0, 6.0, ((0, 4), (2, 32))),
        "reference_features": centred(splits[1], (CH, NPIX), 1.0, 6.0, ((1, 32),)),
        "interp": centred(splits[2], (V, D, TAPS, BLK, BLK), (TAPS * BLK) ** -0.5, 0.375, ((0, 4),)),
        "source_tile": set_ends(jax.random.randint(splits[3], (V, D, NBLK, TAPS), -1, 2), jax.random.fold_in(splits[3], 1), -1, 1).astype(jnp.int32),
        "source_block": set_ends(jax.random.randint(splits[4], (V, D, NBLK, TAPS), 0, NB), jax.random.fold_in(splits[4], 1), 0, NB - 1).astype(jnp.int32),
        "conv_weight": centred(splits[5], (3, 3, 3, OUT_CH, CH), (27 * CH) ** -0.5, 0.21875),
        "grad_regularized": centred(splits[6], (D, OUT_CH, NPIX), 1.0, 6.0, ((0, 4), (2, 32))),
    }


def to_tiles(image):
    lead = image.shape[:-2]
    split = image.reshape(lead + (COLS, N_TILE, ROWS_DEV))
    nd = len(lead)
    moved = jnp.transpose(split, tuple(range(nd)) + (nd + 1, nd + 2, nd))
    return moved.reshape(lead + (N_TILE * ROWS_DEV * COLS,))


def from_tiles(flat):
    lead = flat.shape[:-1]
    split = flat.reshape(lead + (N_TILE, ROWS_DEV, COLS))
    nd = len(lead)
    moved = jnp.transpose(split, tuple(range(nd)) + (nd + 2, nd, nd + 1))
    return moved.reshape(lead + (COLS, N_TILE * ROWS_DEV))


def convolve(padded, conv_weight, count):
    cols = padded.shape[2] - 2
    rows = padded.shape[3] - 2
    result = jnp.zeros((count, conv_weight.shape[3], cols, rows), jnp.float32)
    for plane_tap in range(3):
        for row_tap in range(3):
            for col_tap in range(3):
                part = padded[plane_tap:plane_tap + count, :, col_tap:col_tap + cols, row_tap:row_tap + rows]
                result = result + jnp.einsum("oh,phxy->poxy", conv_weight[plane_tap, row_tap, col_tap].astype(jnp.float32), part.astype(jnp.float32))
    return result


def convolve_back(padded, conv_weight, count):
    cols = padded.shape[2] - 2
    rows = padded.shape[3] - 2
    result = jnp.zeros((count, conv_weight.shape[4], cols, rows), jnp.float32)
    for plane_tap in range(3):
        for row_tap in range(3):
            for col_tap in range(3):
                part = padded[2 - plane_tap:2 - plane_tap + count, :, 2 - col_tap:2 - col_tap + cols, 2 - row_tap:2 - row_tap + rows]
                result = result + jnp.einsum("oh,poxy->phxy", conv_weight[plane_tap, row_tap, col_tap].astype(jnp.float32), part.astype(jnp.float32))
    return result


def reference(source_features, reference_features, interp, source_tile, source_block, conv_weight, grad_regularized):
    blocks_tile = COLS * ROWS_DEV // BLK
    count = float(V + 1)
    tile_of = jnp.arange(NBLK, dtype=jnp.int32) // blocks_tile
    place = (tile_of[None, None, :, None] + source_tile + 1) * blocks_tile + source_block
    place = place.astype(jnp.int32)

    def view_blocks(view_image):
        flat = to_tiles(view_image)
        tiled = flat.reshape(CH, NBLK, BLK).transpose(1, 0, 2)
        rim = jnp.zeros((blocks_tile, CH, BLK), tiled.dtype)
        return jnp.concatenate([rim, tiled, rim], axis=0)

    def warp_plane(blocks, plane_place, plane_interp):
        picked = blocks[plane_place].astype(jnp.float32)
        warped = jnp.einsum("gkci,kij->cgj", picked, plane_interp.astype(jnp.float32))
        return warped.reshape(CH, NPIX)

    def forward_view(carry, inputs):
        image, view_place, view_interp = inputs
        blocks = view_blocks(image)
        warped = lax.map(lambda item: warp_plane(blocks, item[0], item[1]), (view_place, view_interp))
        return (carry[0] + warped, carry[1] + warped * warped), None

    zero_sum = jnp.zeros((D, CH, NPIX), jnp.float32)
    (first_sum, second_sum), unused = lax.scan(forward_view, (zero_sum, zero_sum), (source_features, place, interp))
    ref_float = reference_features.astype(jnp.float32)
    first_sum = first_sum + ref_float
    second_sum = second_sum + ref_float * ref_float
    mean = first_sum / count
    cost = (second_sum / count - mean * mean).astype(jnp.bfloat16)
    cost_image = jnp.pad(from_tiles(cost), ((1, 1), (0, 0), (1, 1), (1, 1)))
    regularized = to_tiles(convolve(cost_image, conv_weight, D)).astype(jnp.bfloat16)

    grad_image = jnp.pad(from_tiles(grad_regularized), ((1, 1), (0, 0), (1, 1), (1, 1)))
    grad_cost = to_tiles(convolve_back(grad_image, conv_weight, D))
    grad_square = (grad_cost / count).astype(jnp.bfloat16)
    grad_mean = (-2.0 * first_sum / (count * count) * grad_cost).astype(jnp.bfloat16)
    segments = (N_TILE + 2) * blocks_tile

    def backward_view(carry, inputs):
        image, view_place, view_interp = inputs
        blocks = view_blocks(image)

        def plane_step(accum, item):
            plane_place, plane_interp, plane_mean, plane_square = item
            warped = warp_plane(blocks, plane_place, plane_interp)
            grad_warped = (plane_mean.astype(jnp.float32) + 2.0 * warped * plane_square.astype(jnp.float32)).astype(jnp.bfloat16)
            spread = jnp.einsum("cgj,kij->gkci", grad_warped.reshape(CH, NBLK, BLK).astype(jnp.float32), plane_interp.astype(jnp.float32))
            landed = jax.ops.segment_sum(spread.reshape(NBLK * TAPS, CH, BLK), plane_place.reshape(-1), num_segments=segments)
            return accum + landed, None

        start_accum = jnp.zeros((segments, CH, BLK), jnp.float32)
        accum, unused_inner = lax.scan(plane_step, start_accum, (view_place, view_interp, grad_mean, grad_square))
        inner = accum[blocks_tile:blocks_tile + NBLK]
        flat = inner.transpose(1, 0, 2).reshape(CH, NPIX)
        return carry, from_tiles(flat)

    unused_carry, grad_source = lax.scan(backward_view, jnp.zeros((), jnp.float32), (source_features, place, interp))
    return regularized, grad_source
```

```python
import functools

import jax
import jax.numpy as jnp
from jax import lax
from jax.experimental import pallas as pl
from jax.experimental.pallas import tpu as pltpu
from jax.sharding import PartitionSpec as P

BF = jnp.bfloat16
F32 = jnp.float32
VIEWS = 5
PLANES = 8
COUNT = 21.0
SEGS = 48
VMEM_LIMIT = 48 * 1024 * 1024
NT = (((1,), (1,)), ((), ()))
NN = (((1,), (0,)), ((), ()))
TN = (((0,), (0,)), ((), ()))


def params():
    return pltpu.CompilerParams(vmem_limit_bytes=VMEM_LIMIT)


def whole():
    return pl.BlockSpec(memory_space=pltpu.VMEM)


def iota(shape, dim):
    return lax.broadcasted_iota(jnp.int32, shape, dim)


def band_table():
    row, lane = iota((96, 128), 0), iota((96, 128), 1)
    return ((lane >> 2) == (row & 31) + (row >> 5) - 1).astype(F32).astype(BF)


def row_mask():
    return (iota((128, 128), 0) >> 5) == (iota((128, 128), 1) & 3)


def strips_kernel(src_ref, out_ref, wide, stage):
    wide[...] = src_ref[...].astype(F32)
    table = band_table()
    mask = row_mask()
    for x in range(8):
        own = wide[pl.ds(x, 160, stride=8), :]
        parts = []
        for v in range(VIEWS):
            part = own[v * 32 : (v + 1) * 32]
            parts.append(jnp.where(mask, jnp.concatenate([part] * 4, axis=0), 0.0).astype(BF))
        stacked = jnp.concatenate(parts, axis=0)
        moved = lax.dot_general(table, stacked, NT, preferred_element_type=F32)
        for v in range(VIEWS):
            for band in range(3):
                stage[v * 3 + band, pl.ds(x, 32, stride=8), :] = moved[
                    band * 32 : (band + 1) * 32, v * 128 : (v + 1) * 128
                ]
    for piece in range(VIEWS * 3):
        out_ref[:, piece * 128 : (piece + 1) * 128] = stage[piece].astype(BF)


def strips(source):
    return pl.pallas_call(
        strips_kernel,
        out_shape=jax.ShapeDtypeStruct((256, VIEWS * 384), BF),
        in_specs=[whole()],
        out_specs=whole(),
        scratch_shapes=[pltpu.VMEM((1280, 128), F32), pltpu.VMEM((VIEWS * 3, 256, 128), F32)],
        compiler_params=params(),
        name="strips",
    )(source)


def unstrips_kernel(in_ref, out_ref, wide):
    for piece in range(VIEWS * 3):
        wide[piece] = in_ref[:, piece * 128 : (piece + 1) * 128].astype(F32)
    table = band_table()
    mask = row_mask()
    for x in range(8):
        columns = []
        for v in range(VIEWS):
            bands = [wide[v * 3 + band, pl.ds(x, 32, stride=8), :] for band in range(3)]
            columns.append(jnp.concatenate(bands, axis=0).astype(BF))
        stacked = jnp.concatenate(columns, axis=1)
        moved = lax.dot_general(stacked, table, TN, preferred_element_type=F32)
        parts = []
        for v in range(VIEWS):
            part = jnp.where(mask, moved[v * 128 : (v + 1) * 128], 0.0)
            parts.append((part[0:32] + part[32:64]) + (part[64:96] + part[96:128]))
        out_ref[pl.ds(x, 160, stride=8), :] = jnp.concatenate(parts, axis=0)


def unstrips(arrived):
    return pl.pallas_call(
        unstrips_kernel,
        out_shape=jax.ShapeDtypeStruct((1280, 128), F32),
        in_specs=[whole()],
        out_specs=whole(),
        scratch_shapes=[pltpu.VMEM((VIEWS * 3, 256, 128), F32)],
        compiler_params=params(),
        name="unstrips",
    )(arrived)


def half_mask(rows):
    return iota((rows, 128), 1) < 64


def spread_interp(values):
    parts = []
    zero = jnp.zeros((64, 64), BF)
    for k in range(4):
        parts.append(jnp.concatenate([values[k], zero], axis=1))
        parts.append(jnp.concatenate([zero, values[k]], axis=1))
    return jnp.concatenate(parts, axis=0)


def pair_swap(low, high):
    mask = half_mask(low.shape[0])
    first = jnp.where(mask, low, pltpu.roll(high, 64, 1))
    second = jnp.where(mask, pltpu.roll(low, 64, 1), high)
    return first, second


def warp_kernel(
    place_ref, order_ref, in_ref, interp_ref, first_o, first_m, second_o, second_m, warped_ref, blocks
):
    view = pl.program_id(0)
    turned = in_ref[...].astype(F32).T
    for band_row in range(12):
        upper = turned[band_row * 32 : band_row * 32 + 16]
        lower = turned[band_row * 32 + 16 : band_row * 32 + 32]
        for half in range(2):
            even, odd = pair_swap(
                upper[:, half * 128 : half * 128 + 128], lower[:, half * 128 : half * 128 + 128]
            )
            blocks[band_row * 4 + half * 2] = even.astype(BF)
            blocks[band_row * 4 + half * 2 + 1] = odd.astype(BF)

    @pl.when(view == 0)
    def _():
        for ref in (first_o, first_m, second_o, second_m):
            ref[...] = jnp.zeros_like(ref)

    for group, (first_ref, second_ref) in enumerate(((first_o, second_o), (first_m, second_m))):

        def step(e, unused, group=group, first_ref=first_ref, second_ref=second_ref):
            plane = order_ref[group * 4 + e]
            base = (view * PLANES + plane) * 64
            rows = []
            for g in range(16):
                taps = [blocks[place_ref[base + g * 4 + k]] for k in range(4)]
                rows.append(jnp.concatenate(taps, axis=1))
            picked = jnp.concatenate(rows, axis=0)
            matrix = spread_interp(interp_ref[0, plane])
            warped = lax.dot_general(picked, matrix, NN, preferred_element_type=F32)
            first_ref[e] += warped
            second_ref[e] += warped * warped
            warped_ref[0, group * 4 + e] = warped.astype(BF)
            return unused

        lax.fori_loop(0, 4, step, 0)


def warp(place, order, arrived, interp):
    sums = jax.ShapeDtypeStruct((4, 256, 128), F32)
    sum_spec = pl.BlockSpec((4, 256, 128), lambda v, p, o: (0, 0, 0))
    return pl.pallas_call(
        warp_kernel,
        grid_spec=pltpu.PrefetchScalarGridSpec(
            num_scalar_prefetch=2,
            grid=(VIEWS,),
            in_specs=[
                pl.BlockSpec((256, 384), lambda v, p, o: (0, v)),
                pl.BlockSpec((1, PLANES, 4, 64, 64), lambda v, p, o: (v, 0, 0, 0, 0)),
            ],
            out_specs=[sum_spec] * 4
            + [pl.BlockSpec((1, PLANES, 256, 128), lambda v, p, o: (v, 0, 0, 0))],
            scratch_shapes=[pltpu.VMEM((SEGS, 16, 128), BF)],
        ),
        out_shape=[sums] * 4 + [jax.ShapeDtypeStruct((VIEWS, PLANES, 256, 128), BF)],
        compiler_params=params(),
        name="warp",
    )(place, order, arrived, interp)


CHAINS = 4


def land_kernel(
    place_ref, order_ref, warped_ref, interp_ref, mean_o, mean_m, grad_ref, out_ref, *accs
):
    view = pl.program_id(0)
    for acc in accs:
        acc[...] = jnp.zeros_like(acc)

    for group, mean_ref in enumerate((mean_o, mean_m)):

        def step(e, unused, group=group, mean_ref=mean_ref):
            plane = order_ref[group * 4 + e]
            base = (view * PLANES + plane) * 64
            warped = warped_ref[0, group * 4 + e].astype(F32)
            grad = (grad_ref[plane] * (warped - mean_ref[e].astype(F32))).astype(BF)
            matrix = spread_interp(interp_ref[0, plane])
            spread = lax.dot_general(grad, matrix, NT, preferred_element_type=F32)
            for g in range(16):
                for k in range(4):
                    where = place_ref[base + g * 4 + k]
                    accs[k][where] += spread[g * 16 : (g + 1) * 16, k * 128 : (k + 1) * 128]
            return unused

        lax.fori_loop(0, 4, step, 0)

    bands = []
    for band_row in range(12):
        columns_up, columns_low = [], []
        for half in range(2):
            at = band_row * 4 + half * 2
            even = (accs[0][at] + accs[1][at]) + (accs[2][at] + accs[3][at])
            odd = (accs[0][at + 1] + accs[1][at + 1]) + (accs[2][at + 1] + accs[3][at + 1])
            up, low = pair_swap(even, odd)
            columns_up.append(up)
            columns_low.append(low)
        bands.append(jnp.concatenate(columns_up, axis=1))
        bands.append(jnp.concatenate(columns_low, axis=1))
    out_ref[...] = jnp.concatenate(bands, axis=0).T.astype(BF)


def land(place, order, warped, interp, mean_other, mean_mine, grad):
    mean_spec = pl.BlockSpec((4, 256, 128), lambda v, p, o: (0, 0, 0))
    return pl.pallas_call(
        land_kernel,
        grid_spec=pltpu.PrefetchScalarGridSpec(
            num_scalar_prefetch=2,
            grid=(VIEWS,),
            in_specs=[
                pl.BlockSpec((1, PLANES, 256, 128), lambda v, p, o: (v, 0, 0, 0)),
                pl.BlockSpec((1, PLANES, 4, 64, 64), lambda v, p, o: (v, 0, 0, 0, 0)),
                mean_spec,
                mean_spec,
                pl.BlockSpec((PLANES, 256, 128), lambda v, p, o: (0, 0, 0)),
            ],
            out_specs=pl.BlockSpec((256, 384), lambda v, p, o: (0, v)),
            scratch_shapes=[pltpu.VMEM((SEGS, 16, 128), F32)] * CHAINS,
        ),
        out_shape=jax.ShapeDtypeStruct((256, VIEWS * 384), BF),
        compiler_params=params(),
        name="land",
    )(place, order, warped, interp, mean_other, mean_mine, grad)


def shifted(values, offset):
    lanes = values.shape[1]
    col = iota(values.shape, 1) & 255
    if offset > 0:
        return jnp.where(col == 255, 0.0, pltpu.roll(values, lanes - 1, 1))
    return jnp.where(col == 0, 0.0, pltpu.roll(values, 1, 1))


def grad_cost_kernel(view_ref, own_ref, top_ref, bottom_ref, weight_ref, out_ref):
    view = view_ref[0]
    padded = []
    for plane in range(PLANES):
        slot = jnp.bitwise_xor(view, plane // 2)
        line = jnp.concatenate(
            [
                top_ref[slot, plane % 2].astype(F32),
                own_ref[slot, plane % 2].astype(F32),
                bottom_ref[slot, plane % 2].astype(F32),
            ],
            axis=1,
        )
        padded.append(jnp.concatenate([shifted(line, 1), line, shifted(line, -1)], axis=0))
    zero = jnp.zeros_like(padded[0])
    weight = weight_ref[...]
    for plane in range(PLANES):
        near = [padded[p] if 0 <= p < PLANES else zero for p in (plane + 1, plane, plane - 1)]
        result = lax.dot_general(
            weight, jnp.concatenate(near, axis=0).astype(BF), NN, preferred_element_type=F32
        )
        grad = result[0:32, 512:1536] + result[32:64, 256:1280] + result[64:96, 0:1024]
        grad = grad * (2.0 / COUNT)
        for pair in range(8):
            upper = grad[0:16, pair * 128 : pair * 128 + 128]
            lower = grad[16:32, pair * 128 : pair * 128 + 128]
            even, odd = pair_swap(upper, lower)
            out_ref[plane, pair * 32 : pair * 32 + 16] = even
            out_ref[plane, pair * 32 + 16 : pair * 32 + 32] = odd


def grad_cost(view, own, top, bottom, weight):
    return pl.pallas_call(
        grad_cost_kernel,
        out_shape=jax.ShapeDtypeStruct((PLANES, 256, 128), F32),
        in_specs=[pl.BlockSpec(memory_space=pltpu.SMEM)] + [whole()] * 4,
        out_specs=whole(),
        compiler_params=params(),
        name="grad_cost",
    )(view, own, top, bottom, weight)


def conv_kernel(below_ref, own_ref, above_ref, top_ref, bottom_ref, weight_ref, out_ref):
    weight = weight_ref[...]
    results = []
    for local in range(4):
        if local == 0:
            middle = below_ref[0]
        elif local == 3:
            middle = above_ref[0]
        else:
            middle = own_ref[local - 1]
        tall = jnp.concatenate([top_ref[local], middle, bottom_ref[local]], axis=0).astype(F32)
        upper, lower = [], []
        for pair in range(12):
            even = tall[pair * 32 : pair * 32 + 16]
            odd = tall[pair * 32 + 16 : pair * 32 + 32]
            up, low = pair_swap(even, odd)
            upper.append(up)
            lower.append(low)
        line = jnp.concatenate(
            [jnp.concatenate(upper, axis=1), jnp.concatenate(lower, axis=1)], axis=0
        )
        wide = jnp.concatenate([shifted(line, -1), line, shifted(line, 1)], axis=0).astype(BF)
        results.append(lax.dot_general(weight, wide, NN, preferred_element_type=F32))
    for plane in range(2):
        total = None
        for a in range(3):
            for b in range(3):
                at = (a * 3 + b) * 8
                part = results[plane + a][at : at + 8, b * 256 : b * 256 + 1024]
                total = part if total is None else total + part
        out_ref[plane] = total.astype(BF)


def conv(below, own, above, top, bottom, weight):
    return pl.pallas_call(
        conv_kernel,
        out_shape=jax.ShapeDtypeStruct((2, 8, 1024), BF),
        in_specs=[whole()] * 6,
        out_specs=whole(),
        compiler_params=params(),
        name="conv",
    )(below, own, above, top, bottom, weight)


def body(
    source_features,
    reference_features,
    interp,
    source_tile,
    source_block,
    conv_weight,
    grad_regularized,
):
    tiles = lax.axis_size("tile")
    views = lax.axis_size("view")
    view = lax.axis_index("view")
    up = [(i, i + 1) for i in range(tiles - 1)]
    down = [(i + 1, i) for i in range(tiles - 1)]

    def other(array, mask):
        return lax.ppermute(array, "view", [(i, i ^ mask) for i in range(views)])

    slots = jnp.arange(8, dtype=jnp.int32)
    y_low, core = view // 2, view % 2
    order = (
        ((slots // 2) % 2 ^ 1 ^ y_low) * 4 + ((slots // 4) ^ 1 ^ core) * 2 + slots % 2
    ).astype(jnp.int32)
    place = ((source_tile + 1) * 16 + source_block).reshape(-1)

    operand = strips(source_features.reshape(1280, 128))
    arrived = lax.all_to_all(operand, "tile", split_axis=0, concat_axis=0, tiled=True)

    own = grad_regularized
    cotangent = jnp.stack([own, other(own, 1), other(own, 2), other(own, 3)])
    top = lax.ppermute(cotangent[..., 768:], "tile", up)
    bottom = lax.ppermute(cotangent[..., :256], "tile", down)
    back_weight = conv_weight.transpose(1, 4, 0, 2, 3).reshape(96, 72)
    grad = grad_cost(view.astype(jnp.int32).reshape(1), cotangent, top, bottom, back_weight)

    first_o, first_m, second_o, second_m, warped = warp(place, order, arrived, interp)
    first_chip = first_m + other(first_o, 1)
    second_chip = second_m + other(second_o, 1)
    first_there = other(first_chip.astype(BF), 2).astype(F32)
    second_there = other(second_chip[:2], 2)
    ref = (
        reference_features.astype(F32).reshape(2, 16, 16, 64).transpose(2, 1, 0, 3).reshape(256, 128)
    )
    first = first_chip + jnp.concatenate([first_there[2:], first_there[:2]], axis=0) + ref
    mean = first / COUNT
    mean_mine = mean.astype(BF)
    mean_other = other(mean_mine, 1)
    second = second_chip[2:] + second_there + ref * ref
    cost = (second / COUNT - mean[2:] * mean[2:]).astype(BF)

    landed = land(place, order, warped, interp, mean_other, mean_mine, grad)
    returned = lax.all_to_all(landed, "tile", split_axis=0, concat_axis=0, tiled=True)

    view_up = [(i, i + 1) for i in range(views - 1)]
    view_down = [(i + 1, i) for i in range(views - 1)]
    below = lax.ppermute(cost[1:], "view", view_up)
    above = lax.ppermute(cost[:1], "view", view_down)
    last = jnp.concatenate([below[:, 192:], cost[:, 192:], above[:, 192:]], axis=0)
    initial = jnp.concatenate([below[:, :64], cost[:, :64], above[:, :64]], axis=0)
    cost_top = lax.ppermute(last, "tile", up)
    cost_bottom = lax.ppermute(initial, "tile", down)
    weight = conv_weight.transpose(0, 1, 3, 2, 4).reshape(72, 96)
    regularized = conv(below, cost, above, cost_top, cost_bottom, weight)

    grad_source = unstrips(returned).reshape(source_features.shape)
    return regularized, grad_source


def solution(mesh):
    return jax.shard_map(
        body,
        mesh=mesh,
        in_specs=(
            P("view", None, "tile", None),
            P(None, "tile"),
            P("view", None, None, None, None),
            P("view", None, "tile", None),
            P("view", None, "tile", None),
            P(),
            P("view", None, "tile"),
        ),
        out_specs=(P("view", None, "tile"), P("view", None, "tile", None)),
        check_vma=False,
    )
```

```python
import functools

import jax
import jax.numpy as jnp
from jax import lax
from jax.experimental import pallas as pl
from jax.experimental.pallas import tpu as pltpu
from jax.sharding import PartitionSpec as P

BF = jnp.bfloat16
F32 = jnp.float32
VIEWS = 5
PLANES = 8
COUNT = 21.0
SEGS = 48
VMEM_LIMIT = 4 * 1024 * 1024
NT = (((1,), (1,)), ((), ()))
NN = (((1,), (0,)), ((), ()))
TN = (((0,), (0,)), ((), ()))


def params():
    return pltpu.CompilerParams(vmem_limit_bytes=VMEM_LIMIT)


def whole():
    return pl.BlockSpec(memory_space=pltpu.VMEM)


def cost_us(microseconds):
    return pl.CostEstimate(
        flops=int(microseconds * 1.0e9), bytes_accessed=int(microseconds * 3.0e6), transcendentals=0
    )


def iota(shape, dim):
    return lax.broadcasted_iota(jnp.int32, shape, dim)


def band_table():
    row, lane = iota((96, 128), 0), iota((96, 128), 1)
    return ((lane >> 2) == (row & 31) + (row >> 5) - 1).astype(F32).astype(BF)


def row_mask():
    return (iota((128, 128), 0) >> 5) == (iota((128, 128), 1) & 3)


def strips_kernel(src_ref, out_ref, wide, stage):
    wide[...] = src_ref[...].astype(F32)
    table = band_table()
    mask = row_mask()
    for x in range(8):
        own = wide[pl.ds(x, 160, stride=8), :]
        parts = []
        for v in range(VIEWS):
            part = own[v * 32 : (v + 1) * 32]
            parts.append(jnp.where(mask, jnp.concatenate([part] * 4, axis=0), 0.0).astype(BF))
        stacked = jnp.concatenate(parts, axis=0)
        moved = lax.dot_general(table, stacked, NT, preferred_element_type=F32)
        for v in range(VIEWS):
            for band in range(3):
                stage[v * 3 + band, pl.ds(x, 32, stride=8), :] = moved[
                    band * 32 : (band + 1) * 32, v * 128 : (v + 1) * 128
                ]
    for piece in range(VIEWS * 3):
        out_ref[:, piece * 128 : (piece + 1) * 128] = stage[piece].astype(BF)


def strips(source):
    return pl.pallas_call(
        strips_kernel,
        out_shape=jax.ShapeDtypeStruct((256, VIEWS * 384), BF),
        in_specs=[whole()],
        out_specs=whole(),
        scratch_shapes=[pltpu.VMEM((1280, 128), F32), pltpu.VMEM((VIEWS * 3, 256, 128), F32)],
        compiler_params=params(),
        name="strips",
    )(source)


def unstrips_kernel(in_ref, out_ref, wide):
    for piece in range(VIEWS * 3):
        wide[piece] = in_ref[:, piece * 128 : (piece + 1) * 128].astype(F32)
    table = band_table()
    mask = row_mask()
    for x in range(8):
        columns = []
        for v in range(VIEWS):
            bands = [wide[v * 3 + band, pl.ds(x, 32, stride=8), :] for band in range(3)]
            columns.append(jnp.concatenate(bands, axis=0).astype(BF))
        stacked = jnp.concatenate(columns, axis=1)
        moved = lax.dot_general(stacked, table, TN, preferred_element_type=F32)
        parts = []
        for v in range(VIEWS):
            part = jnp.where(mask, moved[v * 128 : (v + 1) * 128], 0.0)
            parts.append((part[0:32] + part[32:64]) + (part[64:96] + part[96:128]))
        out_ref[pl.ds(x, 160, stride=8), :] = jnp.concatenate(parts, axis=0)


def unstrips(arrived):
    return pl.pallas_call(
        unstrips_kernel,
        out_shape=jax.ShapeDtypeStruct((1280, 128), F32),
        in_specs=[whole()],
        out_specs=whole(),
        scratch_shapes=[pltpu.VMEM((VIEWS * 3, 256, 128), F32)],
        compiler_params=params(),
        name="unstrips",
    )(arrived)


def half_mask(rows):
    return iota((rows, 128), 1) < 64


def spread_interp(values):
    parts = []
    zero = jnp.zeros((64, 64), BF)
    for k in range(4):
        parts.append(jnp.concatenate([values[k], zero], axis=1))
        parts.append(jnp.concatenate([zero, values[k]], axis=1))
    return jnp.concatenate(parts, axis=0)


def pair_swap(low, high):
    mask = half_mask(low.shape[0])
    first = jnp.where(mask, low, pltpu.roll(high, 64, 1))
    second = jnp.where(mask, pltpu.roll(low, 64, 1), high)
    return first, second


def turn_kernel(in_ref, blocks_ref):
    for view in range(VIEWS):
        turned = in_ref[:, view * 384 : (view + 1) * 384].astype(F32).T
        for band_row in range(12):
            upper = turned[band_row * 32 : band_row * 32 + 16]
            lower = turned[band_row * 32 + 16 : band_row * 32 + 32]
            for half in range(2):
                even, odd = pair_swap(
                    upper[:, half * 128 : half * 128 + 128], lower[:, half * 128 : half * 128 + 128]
                )
                at = view * SEGS + band_row * 4 + half * 2
                blocks_ref[at] = even.astype(BF)
                blocks_ref[at + 1] = odd.astype(BF)


def warp_planes(group, place_ref, order_ref, blocks_ref, interp_ref, first_ref, second_ref, warped_ref):
    first_ref[...] = jnp.zeros_like(first_ref)
    second_ref[...] = jnp.zeros_like(second_ref)

    def step(view, unused):
        for e in range(4):
            plane = order_ref[group * 4 + e]
            base = (view * PLANES + plane) * 64
            rows = []
            for g in range(16):
                taps = [blocks_ref[view * SEGS + place_ref[base + g * 4 + k]] for k in range(4)]
                rows.append(jnp.concatenate(taps, axis=1))
            picked = jnp.concatenate(rows, axis=0)
            matrix = spread_interp(interp_ref[view, plane])
            warped = lax.dot_general(picked, matrix, NN, preferred_element_type=F32)
            first_ref[e] += warped
            second_ref[e] += warped * warped
            warped_ref[view, e] = warped.astype(BF)
        return unused

    lax.fori_loop(0, VIEWS, step, 0, unroll=UNROLL)


def warp_other_kernel(
    place_ref, order_ref, in_ref, interp_ref, blocks_ref, first_ref, second_ref, warped_ref
):
    turn_kernel(in_ref, blocks_ref)
    warp_planes(0, place_ref, order_ref, blocks_ref, interp_ref, first_ref, second_ref, warped_ref)


def warp_mine_kernel(
    place_ref, order_ref, blocks_ref, interp_ref, first_ref, second_ref, warped_ref
):
    warp_planes(1, place_ref, order_ref, blocks_ref, interp_ref, first_ref, second_ref, warped_ref)


UNROLL = 5
SUMS = jax.ShapeDtypeStruct((4, 256, 128), F32)
WARPED = jax.ShapeDtypeStruct((VIEWS, 4, 256, 128), BF)
BLOCKS = jax.ShapeDtypeStruct((VIEWS * SEGS, 16, 128), BF)


def smem():
    return pl.BlockSpec(memory_space=pltpu.SMEM)


def warp_other(place, order, arrived, interp):
    return pl.pallas_call(
        warp_other_kernel,
        in_specs=[smem(), smem(), whole(), whole()],
        out_specs=[whole()] * 4,
        out_shape=[BLOCKS, SUMS, SUMS, WARPED],
        compiler_params=params(),
        name="warp_other",
    )(place, order, arrived, interp)


def warp_mine(place, order, blocks, interp):
    return pl.pallas_call(
        warp_mine_kernel,
        in_specs=[smem(), smem(), whole(), whole()],
        out_specs=[whole()] * 3,
        out_shape=[SUMS, SUMS, WARPED],
        compiler_params=params(),
        name="warp_mine",
    )(place, order, blocks, interp)


CHAINS = 4


def land_views(
    views, place_ref, order_ref, warped_o, warped_m, interp_ref, mean_o, mean_m, grad_ref, out_ref, accs
):
    groups = ((warped_o, mean_o), (warped_m, mean_m))
    for view in views:
        for acc in accs:
            acc[...] = jnp.zeros_like(acc)
        for e in range(8):
            warped_ref, mean_ref = groups[e // 4]
            plane = order_ref[e]
            base = (view * PLANES + plane) * 64
            warped = warped_ref[view, e % 4].astype(F32)
            grad = (grad_ref[plane] * (warped - mean_ref[e % 4].astype(F32))).astype(BF)
            matrix = spread_interp(interp_ref[view, plane])
            spread = lax.dot_general(grad, matrix, NT, preferred_element_type=F32)
            for g in range(16):
                for k in range(4):
                    where = place_ref[base + g * 4 + k]
                    accs[k][where] += spread[g * 16 : (g + 1) * 16, k * 128 : (k + 1) * 128]
        bands = []
        for band_row in range(12):
            columns_up, columns_low = [], []
            for half in range(2):
                at = band_row * 4 + half * 2
                even = (accs[0][at] + accs[1][at]) + (accs[2][at] + accs[3][at])
                odd = (accs[0][at + 1] + accs[1][at + 1]) + (accs[2][at + 1] + accs[3][at + 1])
                up, low = pair_swap(even, odd)
                columns_up.append(up)
                columns_low.append(low)
            bands.append(jnp.concatenate(columns_up, axis=1))
            bands.append(jnp.concatenate(columns_low, axis=1))
        out_ref[:, view * 384 : (view + 1) * 384] = jnp.concatenate(bands, axis=0).T.astype(BF)


def land_first_kernel(views, *refs):
    land_views(views, *refs[:9], refs[9:])


def land_next_kernel(views, *refs):
    land_views(views, *refs[:8], refs[9], refs[10:])


LANDED = jax.ShapeDtypeStruct((256, VIEWS * 384), BF)


def land(views, place, order, warped_o, warped_m, interp, mean_o, mean_m, grad, earlier=None):
    operands = [place, order, warped_o, warped_m, interp, mean_o, mean_m, grad]
    specs = [smem(), smem()] + [whole()] * 6
    if earlier is None:
        kernel, aliases = land_first_kernel, {}
    else:
        kernel, aliases = land_next_kernel, {8: 0}
        operands.append(earlier)
        specs.append(whole())
    return pl.pallas_call(
        functools.partial(kernel, views),
        in_specs=specs,
        out_specs=whole(),
        out_shape=LANDED,
        scratch_shapes=[pltpu.VMEM((SEGS, 16, 128), F32)] * CHAINS,
        input_output_aliases=aliases,
        compiler_params=params(),
        cost_estimate=cost_us(1.4 * len(views)),
        name="land",
    )(*operands)


def chip_first_kernel(mine_ref, arrived_ref, sum_ref, send_ref):
    total = mine_ref[...] + arrived_ref[...]
    sum_ref[...] = total
    send_ref[...] = total.astype(BF)


def chip_second_kernel(where_ref, mine_ref, arrived_ref, own_ref, send_ref):
    core = where_ref[1]
    own_ref[0:2] = mine_ref[2:4] + arrived_ref[2:4]
    own_ref[2] = mine_ref[core] + arrived_ref[core]
    send_ref[0:2] = mine_ref[0:2] + arrived_ref[0:2]
    send_ref[2] = mine_ref[2 + core] + arrived_ref[2 + core]


def chip_first(mine, arrived):
    return pl.pallas_call(
        chip_first_kernel,
        in_specs=[whole()] * 2,
        out_specs=[whole()] * 2,
        out_shape=[SUMS, jax.ShapeDtypeStruct(SUMS.shape, BF)],
        compiler_params=params(),
        name="chip_first",
    )(mine, arrived)


def chip_second(where, mine, arrived):
    return pl.pallas_call(
        chip_second_kernel,
        in_specs=[smem()] + [whole()] * 2,
        out_specs=[whole()] * 2,
        out_shape=[jax.ShapeDtypeStruct((3, 256, 128), F32)] * 2,
        compiler_params=params(),
        name="chip_second",
    )(where, mine, arrived)


def turned_reference(ref_ref, pair):
    lanes = slice(pair * 128, pair * 128 + 128)
    even, odd = pair_swap(ref_ref[0:16, lanes].astype(F32), ref_ref[16:32, lanes].astype(F32))
    return jnp.concatenate([even, odd], axis=0)


def mean_kernel(sum_ref, there_ref, ref_ref, mean_ref):
    for pair in range(8):
        rows = slice(pair * 32, pair * 32 + 32)
        ref = turned_reference(ref_ref, pair)
        for e in range(4):
            total = sum_ref[e, rows] + there_ref[e ^ 2, rows].astype(F32) + ref
            mean_ref[e, rows] = (total * (1.0 / COUNT)).astype(BF)


def mean_of(sums, there, reference):
    return pl.pallas_call(
        mean_kernel,
        in_specs=[whole()] * 3,
        out_specs=whole(),
        out_shape=jax.ShapeDtypeStruct(SUMS.shape, BF),
        compiler_params=params(),
        name="mean",
    )(sums, there, reference)


def cost_kernel(
    where_ref, first_ref, first_there, second_ref, second_there, ref_ref, low_ref, high_ref, send_ref
):
    y_low, core = where_ref[0], where_ref[1]
    inside = jnp.where(y_low == core, 1.0, 0.0)
    for pair in range(8):
        rows = slice(pair * 32, pair * 32 + 32)
        ref = turned_reference(ref_ref, pair)
        square = ref * ref

        def plane_cost(mine, there, slot):
            first = first_ref[mine, rows] + first_there[there, rows].astype(F32) + ref
            second = second_ref[slot, rows] + second_there[slot, rows] + square
            mean = first * (1.0 / COUNT)
            return second * (1.0 / COUNT) - mean * mean

        low = plane_cost(2, 0, 0)
        high = plane_cost(3, 1, 1)
        far = plane_cost(core, 2 + core, 2)
        low_ref[0, rows] = low.astype(BF)
        high_ref[0, rows] = high.astype(BF)
        send_ref[0, rows] = jnp.where(core == 1, low, high).astype(BF)
        send_ref[1, rows] = (far * inside).astype(BF)


def edges_kernel(where_ref, low_ref, high_ref, near_ref, outer_ref, last_ref, initial_ref):
    core = where_ref[1]
    outer_ref[0] = near_ref[1 - core]
    outer_ref[1] = near_ref[core]
    for local, plane in ((0, outer_ref[0]), (1, low_ref[0]), (2, high_ref[0]), (3, outer_ref[1])):
        last_ref[local] = plane[192:256]
        initial_ref[local] = plane[0:64]


PLANE = jax.ShapeDtypeStruct((1, 256, 128), BF)
PAIR = jax.ShapeDtypeStruct((2, 256, 128), BF)
EDGES = jax.ShapeDtypeStruct((4, 64, 128), BF)


def cost_of(where, first, first_there, second, second_there, reference):
    return pl.pallas_call(
        cost_kernel,
        in_specs=[smem()] + [whole()] * 5,
        out_specs=[whole()] * 3,
        out_shape=[PLANE, PLANE, PAIR],
        compiler_params=params(),
        name="cost",
    )(where, first, first_there, second, second_there, reference)


def edges_of(where, low, high, near):
    return pl.pallas_call(
        edges_kernel,
        in_specs=[smem()] + [whole()] * 3,
        out_specs=[whole()] * 3,
        out_shape=[PAIR, EDGES, EDGES],
        compiler_params=params(),
        name="edges",
    )(where, low, high, near)


def slots_kernel(*refs):
    for slot in range(4):
        refs[4][slot] = refs[slot][...]
        refs[5][slot] = refs[slot][:, :, 768:1024]
        refs[6][slot] = refs[slot][:, :, 0:256]


def slots_of(parts):
    row = jax.ShapeDtypeStruct((4, 2, 8, 256), BF)
    return pl.pallas_call(
        slots_kernel,
        in_specs=[whole()] * 4,
        out_specs=[whole()] * 3,
        out_shape=[jax.ShapeDtypeStruct((4, 2, 8, 1024), BF), row, row],
        compiler_params=params(),
        name="slots",
    )(*parts)


def shifted(values, offset):
    lanes = values.shape[1]
    col = iota(values.shape, 1) & 255
    if offset > 0:
        return jnp.where(col == 255, 0.0, pltpu.roll(values, lanes - 1, 1))
    return jnp.where(col == 0, 0.0, pltpu.roll(values, 1, 1))


def grad_cost_kernel(view_ref, own_ref, top_ref, bottom_ref, weight_ref, out_ref):
    view = view_ref[0]
    padded = []
    for plane in range(PLANES):
        slot = jnp.bitwise_xor(view, plane // 2)
        line = jnp.concatenate(
            [
                top_ref[slot, plane % 2].astype(F32),
                own_ref[slot, plane % 2].astype(F32),
                bottom_ref[slot, plane % 2].astype(F32),
            ],
            axis=1,
        )
        padded.append(jnp.concatenate([shifted(line, 1), line, shifted(line, -1)], axis=0))
    zero = jnp.zeros_like(padded[0])
    weight = weight_ref[...]
    for plane in range(PLANES):
        near = [padded[p] if 0 <= p < PLANES else zero for p in (plane + 1, plane, plane - 1)]
        result = lax.dot_general(
            weight, jnp.concatenate(near, axis=0).astype(BF), NN, preferred_element_type=F32
        )
        grad = result[0:32, 512:1536] + result[32:64, 256:1280] + result[64:96, 0:1024]
        grad = grad * (2.0 / COUNT)
        for pair in range(8):
            upper = grad[0:16, pair * 128 : pair * 128 + 128]
            lower = grad[16:32, pair * 128 : pair * 128 + 128]
            even, odd = pair_swap(upper, lower)
            out_ref[plane, pair * 32 : pair * 32 + 16] = even
            out_ref[plane, pair * 32 + 16 : pair * 32 + 32] = odd


def grad_cost(view, own, top, bottom, weight):
    return pl.pallas_call(
        grad_cost_kernel,
        out_shape=jax.ShapeDtypeStruct((PLANES, 256, 128), F32),
        in_specs=[pl.BlockSpec(memory_space=pltpu.SMEM)] + [whole()] * 4,
        out_specs=whole(),
        compiler_params=params(),
        name="grad_cost",
    )(view, own, top, bottom, weight)


def conv_kernel(outer_ref, low_ref, high_ref, top_ref, bottom_ref, weight_ref, out_ref):
    weight = weight_ref[...]
    results = []
    for local in range(4):
        middle = (outer_ref, low_ref, high_ref, outer_ref)[local][1 if local == 3 else 0]
        tall = jnp.concatenate([top_ref[local], middle, bottom_ref[local]], axis=0).astype(F32)
        upper, lower = [], []
        for pair in range(12):
            even = tall[pair * 32 : pair * 32 + 16]
            odd = tall[pair * 32 + 16 : pair * 32 + 32]
            up, low = pair_swap(even, odd)
            upper.append(up)
            lower.append(low)
        line = jnp.concatenate(
            [jnp.concatenate(upper, axis=1), jnp.concatenate(lower, axis=1)], axis=0
        )
        wide = jnp.concatenate([shifted(line, -1), line, shifted(line, 1)], axis=0).astype(BF)
        results.append(lax.dot_general(weight, wide, NN, preferred_element_type=F32))
    for plane in range(2):
        total = None
        for a in range(3):
            for b in range(3):
                at = (a * 3 + b) * 8
                part = results[plane + a][at : at + 8, b * 256 : b * 256 + 1024]
                total = part if total is None else total + part
        out_ref[plane] = total.astype(BF)


def conv(outer, low, high, top, bottom, weight):
    return pl.pallas_call(
        conv_kernel,
        out_shape=jax.ShapeDtypeStruct((2, 8, 1024), BF),
        in_specs=[whole()] * 6,
        out_specs=whole(),
        compiler_params=params(),
        name="conv",
    )(outer, low, high, top, bottom, weight)


def body(
    source_features,
    reference_features,
    interp,
    source_tile,
    source_block,
    conv_weight,
    grad_regularized,
):
    tiles = lax.axis_size("tile")
    views = lax.axis_size("view")
    view = lax.axis_index("view")
    up = [(i, i + 1) for i in range(tiles - 1)]
    down = [(i + 1, i) for i in range(tiles - 1)]

    def other(array, mask):
        return lax.ppermute(array, "view", [(i, i ^ mask) for i in range(views)])

    slots = jnp.arange(8, dtype=jnp.int32)
    y_low, core = view // 2, view % 2
    order = (
        ((slots // 2) % 2 ^ 1 ^ y_low) * 4 + ((slots // 4) ^ 1 ^ core) * 2 + slots % 2
    ).astype(jnp.int32)
    place = ((source_tile + 1) * 16 + source_block).reshape(-1)

    where = jnp.stack([y_low, core]).astype(jnp.int32)
    own = grad_regularized
    parts = (own, other(own, 1), other(own, 2), other(own, 3))
    operand = strips(source_features.reshape(1280, 128))
    cotangent, last, initial = slots_of(parts)
    operand, last, initial = lax.optimization_barrier((operand, last, initial))
    arrived = lax.all_to_all(operand, "tile", split_axis=0, concat_axis=0, tiled=True)
    top = lax.ppermute(last, "tile", up)
    bottom = lax.ppermute(initial, "tile", down)
    back_weight = conv_weight.transpose(1, 4, 0, 2, 3).reshape(96, 72)
    weight = conv_weight.transpose(0, 1, 3, 2, 4).reshape(72, 96)
    grad = grad_cost(view.astype(jnp.int32).reshape(1), cotangent, top, bottom, back_weight)
    arrived, grad, weight = lax.optimization_barrier((arrived, grad, weight))

    blocks, first_o, second_o, warped_o = warp_other(place, order, arrived, interp)
    first_m, second_m, warped_m = warp_mine(place, order, blocks, interp)
    first_chip, first_send = chip_first(first_m, other(first_o, 1))
    first_there = other(first_send, 2)
    second_own, second_send = chip_second(where, second_m, other(second_o, 1))
    second_there = other(second_send, 2)
    first_there, second_own = lax.optimization_barrier((first_there, second_own))
    mean_mine = mean_of(first_chip, first_there, reference_features)
    mean_other = other(mean_mine, 1)

    shared = (place, order, warped_o, warped_m, interp, mean_other, mean_mine, grad)
    landed = land((0, 1, 2), *shared)
    landed, second_there = lax.optimization_barrier((landed, second_there))
    low, high, send = cost_of(
        where, first_chip, first_there, second_own, second_there, reference_features
    )
    near = other(send, 1)
    landed = land((3, 4), *shared, landed)
    landed, near = lax.optimization_barrier((landed, near))
    outer, cost_last, cost_initial = edges_of(where, low, high, near)
    landed, cost_last, cost_initial = lax.optimization_barrier((landed, cost_last, cost_initial))
    returned = lax.all_to_all(landed, "tile", split_axis=0, concat_axis=0, tiled=True)
    cost_top = lax.ppermute(cost_last, "tile", up)
    cost_bottom = lax.ppermute(cost_initial, "tile", down)
    regularized = conv(outer, low, high, cost_top, cost_bottom, weight)

    grad_source = unstrips(returned).reshape(source_features.shape)
    return regularized, grad_source


def solution(mesh):
    return jax.shard_map(
        body,
        mesh=mesh,
        in_specs=(
            P("view", None, "tile", None),
            P(None, "tile"),
            P("view", None, None, None, None),
            P("view", None, "tile", None),
            P("view", None, "tile", None),
            P(),
            P("view", None, "tile"),
        ),
        out_specs=(P("view", None, "tile"), P("view", None, "tile", None)),
        check_vma=False,
    )
```

```python
import functools

import jax
import jax.numpy as jnp
from jax import lax
from jax.experimental import pallas as pl
from jax.experimental.pallas import tpu as pltpu
from jax.sharding import PartitionSpec as P

BF = jnp.bfloat16
F32 = jnp.float32
VIEWS = 5
PLANES = 8
COUNT = 21.0
SEGS = 48
VMEM_LIMIT = 8 * 1024 * 1024
NT = (((1,), (1,)), ((), ()))
NN = (((1,), (0,)), ((), ()))
TN = (((0,), (0,)), ((), ()))


def params():
    return pltpu.CompilerParams(vmem_limit_bytes=VMEM_LIMIT)


def whole():
    return pl.BlockSpec(memory_space=pltpu.VMEM)


SMALL = pl.CostEstimate(flops=1000, bytes_accessed=1000, transcendentals=0)


def iota(shape, dim):
    return lax.broadcasted_iota(jnp.int32, shape, dim)


def band_table():
    row, lane = iota((96, 128), 0), iota((96, 128), 1)
    return ((lane >> 2) == (row & 31) + (row >> 5) - 1).astype(F32).astype(BF)


def row_mask():
    return (iota((128, 128), 0) >> 5) == (iota((128, 128), 1) & 3)


def strips_kernel(src_ref, out_ref, wide, stage):
    wide[...] = src_ref[...].astype(F32)
    table = band_table()
    mask = row_mask()
    for x in range(8):
        own = wide[pl.ds(x, 32, stride=8), :]
        tall = jnp.where(mask, jnp.concatenate([own] * 4, axis=0), 0.0).astype(BF)
        moved = lax.dot_general(table, tall, NT, preferred_element_type=F32)
        for band in range(3):
            stage[band, pl.ds(x, 32, stride=8), :] = moved[band * 32 : (band + 1) * 32]
    for band in range(3):
        out_ref[:, band * 128 : (band + 1) * 128] = stage[band].astype(BF)


def strips(source):
    return pl.pallas_call(
        strips_kernel,
        grid=(VIEWS,),
        out_shape=pltpu.HBM((256, VIEWS * 384), BF),
        in_specs=[pl.BlockSpec((256, 128), lambda v: (v, 0))],
        out_specs=pl.BlockSpec((256, 384), lambda v: (0, v)),
        scratch_shapes=[pltpu.VMEM((256, 128), F32), pltpu.VMEM((3, 256, 128), F32)],
        compiler_params=params(),
        name="strips",
    )(source)


def unstrips_kernel(in_ref, out_ref, wide):
    for piece in range(VIEWS * 3):
        wide[piece] = in_ref[:, piece * 128 : (piece + 1) * 128].astype(F32)
    table = band_table()
    mask = row_mask()
    for x in range(8):
        columns = []
        for v in range(VIEWS):
            bands = [wide[v * 3 + band, pl.ds(x, 32, stride=8), :] for band in range(3)]
            columns.append(jnp.concatenate(bands, axis=0).astype(BF))
        stacked = jnp.concatenate(columns, axis=1)
        moved = lax.dot_general(stacked, table, TN, preferred_element_type=F32)
        parts = []
        for v in range(VIEWS):
            part = jnp.where(mask, moved[v * 128 : (v + 1) * 128], 0.0)
            parts.append((part[0:32] + part[32:64]) + (part[64:96] + part[96:128]))
        out_ref[pl.ds(x, 160, stride=8), :] = jnp.concatenate(parts, axis=0)


def unstrips(arrived):
    return pl.pallas_call(
        unstrips_kernel,
        out_shape=jax.ShapeDtypeStruct((1280, 128), F32),
        in_specs=[whole()],
        out_specs=whole(),
        scratch_shapes=[pltpu.VMEM((VIEWS * 3, 256, 128), F32)],
        compiler_params=params(),
        name="unstrips",
    )(arrived)


def half_mask(rows):
    return iota((rows, 128), 1) < 64


def spread_interp(values):
    parts = []
    zero = jnp.zeros((64, 64), BF)
    for k in range(4):
        parts.append(jnp.concatenate([values[k], zero], axis=1))
        parts.append(jnp.concatenate([zero, values[k]], axis=1))
    return jnp.concatenate(parts, axis=0)


def pair_swap(low, high):
    mask = half_mask(low.shape[0])
    first = jnp.where(mask, low, pltpu.roll(high, 64, 1))
    second = jnp.where(mask, pltpu.roll(low, 64, 1), high)
    return first, second


def turn_kernel(in_ref, blocks_ref):
    for view in range(VIEWS):
        turned = in_ref[:, view * 384 : (view + 1) * 384].astype(F32).T
        for band_row in range(12):
            upper = turned[band_row * 32 : band_row * 32 + 16]
            lower = turned[band_row * 32 + 16 : band_row * 32 + 32]
            for half in range(2):
                even, odd = pair_swap(
                    upper[:, half * 128 : half * 128 + 128], lower[:, half * 128 : half * 128 + 128]
                )
                at = view * SEGS + band_row * 4 + half * 2
                blocks_ref[at] = even.astype(BF)
                blocks_ref[at + 1] = odd.astype(BF)


def warp_planes(group, place_ref, order_ref, blocks_ref, interp_hbm, first_ref, second_ref,
                warped_hbm, interp_ref, warped_ref, in_sem, out_sem, prepare):
    loads = []
    for view in range(VIEWS):
        for pair in range(2):
            plane = order_ref[group * 4 + pair * 2]
            loads.append(
                pltpu.make_async_copy(
                    interp_hbm.at[view, pl.ds(plane, 2)],
                    interp_ref.at[view, pl.ds(pair * 2, 2)],
                    in_sem.at[view, pair],
                )
            )
    for load in loads:
        load.start()
    prepare()
    first_ref[...] = jnp.zeros_like(first_ref)
    second_ref[...] = jnp.zeros_like(second_ref)
    stores = []
    for view in range(VIEWS):
        for e in range(4):
            if e % 2 == 0:
                loads[view * 2 + e // 2].wait()
            plane = order_ref[group * 4 + e]
            base = (view * PLANES + plane) * 64
            rows = []
            for g in range(16):
                taps = [blocks_ref[view * SEGS + place_ref[base + g * 4 + k]] for k in range(4)]
                rows.append(jnp.concatenate(taps, axis=1))
            picked = jnp.concatenate(rows, axis=0)
            matrix = spread_interp(interp_ref[view, e])
            warped = lax.dot_general(picked, matrix, NN, preferred_element_type=F32)
            first_ref[e] += warped
            second_ref[e] += warped * warped
            warped_ref[view, e] = warped.astype(BF)
        store = pltpu.make_async_copy(warped_ref.at[view], warped_hbm.at[view], out_sem.at[view])
        store.start()
        stores.append(store)
    for store in stores:
        store.wait()


def warp_other_kernel(
    place_ref, order_ref, in_ref, interp_hbm, blocks_ref, first_ref, second_ref, *rest
):
    warp_planes(
        0, place_ref, order_ref, blocks_ref, interp_hbm, first_ref, second_ref, *rest,
        lambda: turn_kernel(in_ref, blocks_ref),
    )


def warp_mine_kernel(place_ref, order_ref, blocks_ref, interp_hbm, first_ref, second_ref, *rest):
    warp_planes(
        1, place_ref, order_ref, blocks_ref, interp_hbm, first_ref, second_ref, *rest, lambda: None
    )


SUMS = jax.ShapeDtypeStruct((4, 256, 128), F32)
WARPED = pltpu.HBM((VIEWS, 4, 256, 128), BF)
BLOCKS = jax.ShapeDtypeStruct((VIEWS * SEGS, 16, 128), BF)


def smem():
    return pl.BlockSpec(memory_space=pltpu.SMEM)


def in_hbm(array):
    return pltpu.with_memory_space_constraint(array, pltpu.HBM)


def hbm():
    return pl.BlockSpec(memory_space=pltpu.HBM)


WARP_SCRATCH = [
    pltpu.VMEM((VIEWS, 4, 4, 64, 64), BF),
    pltpu.VMEM((VIEWS, 4, 256, 128), BF),
    pltpu.SemaphoreType.DMA((VIEWS, 2)),
    pltpu.SemaphoreType.DMA((VIEWS,)),
]


def warp_other(place, order, arrived, interp):
    return pl.pallas_call(
        warp_other_kernel,
        in_specs=[smem(), smem(), whole(), hbm()],
        out_specs=[whole()] * 3 + [hbm()],
        scratch_shapes=WARP_SCRATCH,
        out_shape=[BLOCKS, SUMS, SUMS, WARPED],
        compiler_params=params(),
        name="warp_other",
    )(place, order, arrived, in_hbm(interp))


def warp_mine(place, order, blocks, interp):
    return pl.pallas_call(
        warp_mine_kernel,
        in_specs=[smem(), smem(), whole(), hbm()],
        out_specs=[whole()] * 2 + [hbm()],
        scratch_shapes=WARP_SCRATCH,
        out_shape=[SUMS, SUMS, WARPED],
        compiler_params=params(),
        name="warp_mine",
    )(place, order, blocks, in_hbm(interp))


CHAINS = 4


def land_kernel(views, aliased, place_ref, order_ref, warped_o, warped_m, interp_hbm, mean_o, mean_m,
                grad_ref, *rest):
    out_hbm, warped_ref, interp_ref, out_ref, in_sem, out_sem, *accs = rest[aliased:]
    loads = []
    for at, view in enumerate(views):
        loads.append(
            [
                pltpu.make_async_copy(interp_hbm.at[view], interp_ref.at[at], in_sem.at[at, 0]),
                pltpu.make_async_copy(
                    warped_o.at[view], warped_ref.at[at, pl.ds(0, 4)], in_sem.at[at, 1]
                ),
                pltpu.make_async_copy(
                    warped_m.at[view], warped_ref.at[at, pl.ds(4, 4)], in_sem.at[at, 2]
                ),
            ]
        )
    for load in loads:
        for copy in load:
            copy.start()
    stores = []
    for at, view in enumerate(views):
        for acc in accs:
            acc[...] = jnp.zeros_like(acc)
        for copy in loads[at]:
            copy.wait()
        for e in range(8):
            mean_ref = (mean_o, mean_m)[e // 4]
            plane = order_ref[e]
            base = (view * PLANES + plane) * 64
            warped = warped_ref[at, e].astype(F32)
            grad = (grad_ref[plane] * (warped - mean_ref[e % 4].astype(F32))).astype(BF)
            matrix = spread_interp(interp_ref[at, plane])
            spread = lax.dot_general(grad, matrix, NT, preferred_element_type=F32)
            for g in range(16):
                for k in range(4):
                    where = place_ref[base + g * 4 + k]
                    accs[k][where] += spread[g * 16 : (g + 1) * 16, k * 128 : (k + 1) * 128]
        bands = []
        for band_row in range(12):
            columns_up, columns_low = [], []
            for half in range(2):
                seg = band_row * 4 + half * 2
                even = (accs[0][seg] + accs[1][seg]) + (accs[2][seg] + accs[3][seg])
                odd = (accs[0][seg + 1] + accs[1][seg + 1]) + (accs[2][seg + 1] + accs[3][seg + 1])
                up, low = pair_swap(even, odd)
                columns_up.append(up)
                columns_low.append(low)
            bands.append(jnp.concatenate(columns_up, axis=1))
            bands.append(jnp.concatenate(columns_low, axis=1))
        out_ref[at] = jnp.concatenate(bands, axis=0).T.astype(BF)
        store = pltpu.make_async_copy(
            out_ref.at[at], out_hbm.at[:, view * 384 : (view + 1) * 384], out_sem.at[at]
        )
        store.start()
        stores.append(store)
    for store in stores:
        store.wait()


LANDED = pltpu.HBM((256, VIEWS * 384), BF)


def land(views, place, order, warped_o, warped_m, interp, mean_o, mean_m, grad, earlier=None):
    warped_o, warped_m, interp = (in_hbm(a) for a in (warped_o, warped_m, interp))
    operands = [place, order, warped_o, warped_m, interp, mean_o, mean_m, grad]
    specs = [smem(), smem(), hbm(), hbm(), hbm(), whole(), whole(), whole()]
    aliased = 0 if earlier is None else 1
    if aliased:
        operands.append(earlier)
        specs.append(hbm())
    count = len(views)
    return pl.pallas_call(
        functools.partial(land_kernel, views, aliased),
        in_specs=specs,
        out_specs=hbm(),
        out_shape=LANDED,
        scratch_shapes=[
            pltpu.VMEM((count, PLANES, 256, 128), BF),
            pltpu.VMEM((count, PLANES, 4, 64, 64), BF),
            pltpu.VMEM((count, 256, 384), BF),
            pltpu.SemaphoreType.DMA((count, 3)),
            pltpu.SemaphoreType.DMA((count,)),
        ]
        + [pltpu.VMEM((SEGS, 16, 128), F32)] * CHAINS,
        input_output_aliases={8: 0} if aliased else {},
        compiler_params=params(),
        cost_estimate=SMALL,
        name="land",
    )(*operands)


def chip_first_kernel(mine_ref, arrived_ref, sum_ref, send_ref):
    total = mine_ref[...] + arrived_ref[...]
    sum_ref[...] = total
    send_ref[...] = total.astype(BF)


def chip_second_kernel(where_ref, mine_ref, arrived_ref, own_ref, send_ref):
    core = where_ref[1]
    own_ref[0:2] = mine_ref[2:4] + arrived_ref[2:4]
    own_ref[2] = mine_ref[core] + arrived_ref[core]
    send_ref[0:2] = mine_ref[0:2] + arrived_ref[0:2]
    send_ref[2] = mine_ref[2 + core] + arrived_ref[2 + core]


def chip_first(mine, arrived):
    return pl.pallas_call(
        chip_first_kernel,
        in_specs=[whole()] * 2,
        out_specs=[whole()] * 2,
        out_shape=[SUMS, jax.ShapeDtypeStruct(SUMS.shape, BF)],
        compiler_params=params(),
        name="chip_first",
    )(mine, arrived)


def chip_second(where, mine, arrived):
    return pl.pallas_call(
        chip_second_kernel,
        in_specs=[smem()] + [whole()] * 2,
        out_specs=[whole()] * 2,
        out_shape=[jax.ShapeDtypeStruct((3, 256, 128), F32)] * 2,
        compiler_params=params(),
        name="chip_second",
    )(where, mine, arrived)


def turned_reference(ref_ref, pair):
    lanes = slice(pair * 128, pair * 128 + 128)
    even, odd = pair_swap(ref_ref[0:16, lanes].astype(F32), ref_ref[16:32, lanes].astype(F32))
    return jnp.concatenate([even, odd], axis=0)


def mean_kernel(sum_ref, there_ref, ref_ref, mean_ref):
    for pair in range(8):
        rows = slice(pair * 32, pair * 32 + 32)
        ref = turned_reference(ref_ref, pair)
        for e in range(4):
            total = sum_ref[e, rows] + there_ref[e ^ 2, rows].astype(F32) + ref
            mean_ref[e, rows] = (total * (1.0 / COUNT)).astype(BF)


def mean_of(sums, there, reference):
    return pl.pallas_call(
        mean_kernel,
        in_specs=[whole()] * 3,
        out_specs=whole(),
        out_shape=jax.ShapeDtypeStruct(SUMS.shape, BF),
        compiler_params=params(),
        name="mean",
    )(sums, there, reference)


def cost_kernel(
    where_ref, first_ref, first_there, second_ref, second_there, ref_ref, low_ref, high_ref, send_ref
):
    y_low, core = where_ref[0], where_ref[1]
    inside = jnp.where(y_low == core, 1.0, 0.0)
    for pair in range(8):
        rows = slice(pair * 32, pair * 32 + 32)
        ref = turned_reference(ref_ref, pair)
        square = ref * ref

        def plane_cost(mine, there, slot):
            first = first_ref[mine, rows] + first_there[there, rows].astype(F32) + ref
            second = second_ref[slot, rows] + second_there[slot, rows] + square
            mean = first * (1.0 / COUNT)
            return second * (1.0 / COUNT) - mean * mean

        low = plane_cost(2, 0, 0)
        high = plane_cost(3, 1, 1)
        far = plane_cost(core, 2 + core, 2)
        low_ref[0, rows] = low.astype(BF)
        high_ref[0, rows] = high.astype(BF)
        send_ref[0, rows] = jnp.where(core == 1, low, high).astype(BF)
        send_ref[1, rows] = (far * inside).astype(BF)


def edges_kernel(where_ref, low_ref, high_ref, near_ref, outer_ref, last_ref, initial_ref):
    core = where_ref[1]
    outer_ref[0] = near_ref[1 - core]
    outer_ref[1] = near_ref[core]
    for local, plane in ((0, outer_ref[0]), (1, low_ref[0]), (2, high_ref[0]), (3, outer_ref[1])):
        last_ref[local] = plane[192:256]
        initial_ref[local] = plane[0:64]


PLANE = jax.ShapeDtypeStruct((1, 256, 128), BF)
PAIR = jax.ShapeDtypeStruct((2, 256, 128), BF)
EDGES = jax.ShapeDtypeStruct((4, 64, 128), BF)


def cost_of(where, first, first_there, second, second_there, reference):
    return pl.pallas_call(
        cost_kernel,
        in_specs=[smem()] + [whole()] * 5,
        out_specs=[whole()] * 3,
        out_shape=[PLANE, PLANE, PAIR],
        compiler_params=params(),
        name="cost",
    )(where, first, first_there, second, second_there, reference)


def edges_of(where, low, high, near):
    return pl.pallas_call(
        edges_kernel,
        in_specs=[smem()] + [whole()] * 3,
        out_specs=[whole()] * 3,
        out_shape=[PAIR, EDGES, EDGES],
        compiler_params=params(),
        name="edges",
    )(where, low, high, near)


def slots_kernel(*refs):
    for slot in range(4):
        refs[4][slot] = refs[slot][...]
        refs[5][slot] = refs[slot][:, :, 768:1024]
        refs[6][slot] = refs[slot][:, :, 0:256]


def slots_of(parts):
    row = jax.ShapeDtypeStruct((4, 2, 8, 256), BF)
    return pl.pallas_call(
        slots_kernel,
        in_specs=[whole()] * 4,
        out_specs=[whole()] * 3,
        out_shape=[jax.ShapeDtypeStruct((4, 2, 8, 1024), BF), row, row],
        compiler_params=params(),
        name="slots",
    )(*parts)


def shifted(values, offset):
    lanes = values.shape[1]
    col = iota(values.shape, 1) & 255
    if offset > 0:
        return jnp.where(col == 255, 0.0, pltpu.roll(values, lanes - 1, 1))
    return jnp.where(col == 0, 0.0, pltpu.roll(values, 1, 1))


def grad_cost_kernel(view_ref, own_ref, top_ref, bottom_ref, weight_ref, out_ref):
    view = view_ref[0]
    padded = []
    for plane in range(PLANES):
        slot = jnp.bitwise_xor(view, plane // 2)
        line = jnp.concatenate(
            [
                top_ref[slot, plane % 2].astype(F32),
                own_ref[slot, plane % 2].astype(F32),
                bottom_ref[slot, plane % 2].astype(F32),
            ],
            axis=1,
        )
        padded.append(jnp.concatenate([shifted(line, 1), line, shifted(line, -1)], axis=0))
    zero = jnp.zeros_like(padded[0])
    weight = weight_ref[...]
    for plane in range(PLANES):
        near = [padded[p] if 0 <= p < PLANES else zero for p in (plane + 1, plane, plane - 1)]
        result = lax.dot_general(
            weight, jnp.concatenate(near, axis=0).astype(BF), NN, preferred_element_type=F32
        )
        grad = result[0:32, 512:1536] + result[32:64, 256:1280] + result[64:96, 0:1024]
        grad = grad * (2.0 / COUNT)
        for pair in range(8):
            upper = grad[0:16, pair * 128 : pair * 128 + 128]
            lower = grad[16:32, pair * 128 : pair * 128 + 128]
            even, odd = pair_swap(upper, lower)
            out_ref[plane, pair * 32 : pair * 32 + 16] = even
            out_ref[plane, pair * 32 + 16 : pair * 32 + 32] = odd


def grad_cost(view, own, top, bottom, weight):
    return pl.pallas_call(
        grad_cost_kernel,
        out_shape=jax.ShapeDtypeStruct((PLANES, 256, 128), F32),
        in_specs=[pl.BlockSpec(memory_space=pltpu.SMEM)] + [whole()] * 4,
        out_specs=whole(),
        compiler_params=params(),
        name="grad_cost",
    )(view, own, top, bottom, weight)


def conv_kernel(outer_ref, low_ref, high_ref, top_ref, bottom_ref, weight_ref, out_ref):
    weight = weight_ref[...]
    results = []
    for local in range(4):
        middle = (outer_ref, low_ref, high_ref, outer_ref)[local][1 if local == 3 else 0]
        tall = jnp.concatenate([top_ref[local], middle, bottom_ref[local]], axis=0).astype(F32)
        upper, lower = [], []
        for pair in range(12):
            even = tall[pair * 32 : pair * 32 + 16]
            odd = tall[pair * 32 + 16 : pair * 32 + 32]
            up, low = pair_swap(even, odd)
            upper.append(up)
            lower.append(low)
        line = jnp.concatenate(
            [jnp.concatenate(upper, axis=1), jnp.concatenate(lower, axis=1)], axis=0
        )
        wide = jnp.concatenate([shifted(line, -1), line, shifted(line, 1)], axis=0).astype(BF)
        results.append(lax.dot_general(weight, wide, NN, preferred_element_type=F32))
    for plane in range(2):
        total = None
        for a in range(3):
            for b in range(3):
                at = (a * 3 + b) * 8
                part = results[plane + a][at : at + 8, b * 256 : b * 256 + 1024]
                total = part if total is None else total + part
        out_ref[plane] = total.astype(BF)


def conv(outer, low, high, top, bottom, weight):
    return pl.pallas_call(
        conv_kernel,
        out_shape=jax.ShapeDtypeStruct((2, 8, 1024), BF),
        in_specs=[whole()] * 6,
        out_specs=whole(),
        compiler_params=params(),
        name="conv",
    )(outer, low, high, top, bottom, weight)


def body(
    source_features,
    reference_features,
    interp,
    source_tile,
    source_block,
    conv_weight,
    grad_regularized,
):
    tiles = lax.axis_size("tile")
    views = lax.axis_size("view")
    view = lax.axis_index("view")
    up = [(i, i + 1) for i in range(tiles - 1)]
    down = [(i + 1, i) for i in range(tiles - 1)]

    def other(array, mask):
        return lax.ppermute(array, "view", [(i, i ^ mask) for i in range(views)])

    slots = jnp.arange(8, dtype=jnp.int32)
    y_low, core = view // 2, view % 2
    order = (
        ((slots // 2) % 2 ^ 1 ^ y_low) * 4 + ((slots // 4) ^ 1 ^ core) * 2 + slots % 2
    ).astype(jnp.int32)
    place = ((source_tile + 1) * 16 + source_block).reshape(-1)

    where = jnp.stack([y_low, core]).astype(jnp.int32)
    own = grad_regularized
    parts = (own, other(own, 1), other(own, 2), other(own, 3))
    operand = strips(source_features.reshape(1280, 128))
    cotangent, last, initial = slots_of(parts)
    operand, last, initial = lax.optimization_barrier((operand, last, initial))
    arrived = lax.all_to_all(operand, "tile", split_axis=0, concat_axis=0, tiled=True)
    top = lax.ppermute(last, "tile", up)
    bottom = lax.ppermute(initial, "tile", down)
    back_weight = conv_weight.transpose(1, 4, 0, 2, 3).reshape(96, 72)
    weight = conv_weight.transpose(0, 1, 3, 2, 4).reshape(72, 96)
    arrived, top, bottom, weight, back_weight = lax.optimization_barrier(
        (arrived, top, bottom, weight, back_weight)
    )

    blocks, first_o, second_o, warped_o = warp_other(place, order, arrived, interp)
    first_m, second_m, warped_m = warp_mine(place, order, blocks, interp)
    first_chip, first_send = chip_first(first_m, other(first_o, 1))
    first_there = other(first_send, 2)
    second_own, second_send = chip_second(where, second_m, other(second_o, 1))
    second_there = other(second_send, 2)
    grad = grad_cost(view.astype(jnp.int32).reshape(1), cotangent, top, bottom, back_weight)
    first_there, second_own, grad = lax.optimization_barrier((first_there, second_own, grad))
    mean_mine = mean_of(first_chip, first_there, reference_features)
    mean_other = other(mean_mine, 1)

    shared = (place, order, warped_o, warped_m, interp, mean_other, mean_mine, grad)
    landed = land((0, 1, 2), *shared)
    landed, second_there = lax.optimization_barrier((landed, second_there))
    low, high, send = cost_of(
        where, first_chip, first_there, second_own, second_there, reference_features
    )
    near = other(send, 1)
    landed = land((3, 4), *shared, landed)
    landed, near = lax.optimization_barrier((landed, near))
    outer, cost_last, cost_initial = edges_of(where, low, high, near)
    landed, cost_last, cost_initial = lax.optimization_barrier((landed, cost_last, cost_initial))
    returned = lax.all_to_all(landed, "tile", split_axis=0, concat_axis=0, tiled=True)
    cost_top = lax.ppermute(cost_last, "tile", up)
    cost_bottom = lax.ppermute(cost_initial, "tile", down)
    regularized = conv(outer, low, high, cost_top, cost_bottom, weight)

    grad_source = unstrips(returned).reshape(source_features.shape)
    return regularized, grad_source


def solution(mesh):
    return jax.shard_map(
        body,
        mesh=mesh,
        in_specs=(
            P("view", None, "tile", None),
            P(None, "tile"),
            P("view", None, None, None, None),
            P("view", None, "tile", None),
            P("view", None, "tile", None),
            P(),
            P("view", None, "tile"),
        ),
        out_specs=(P("view", None, "tile"), P("view", None, "tile", None)),
        check_vma=False,
    )
```

```python
import functools

import jax
import jax.numpy as jnp
from jax import lax
from jax.experimental import pallas as pl
from jax.experimental.pallas import tpu as pltpu
from jax.sharding import PartitionSpec as P

BF = jnp.bfloat16
F32 = jnp.float32
VIEWS = 5
PLANES = 8
COUNT = 21.0
SEGS = 48
VMEM_LIMIT = 4 * 1024 * 1024
NT = (((1,), (1,)), ((), ()))
NN = (((1,), (0,)), ((), ()))
TN = (((0,), (0,)), ((), ()))


def params():
    return pltpu.CompilerParams(vmem_limit_bytes=VMEM_LIMIT)


def whole():
    return pl.BlockSpec(memory_space=pltpu.VMEM)


SMALL = pl.CostEstimate(flops=1000, bytes_accessed=1000, transcendentals=0)


def iota(shape, dim):
    return lax.broadcasted_iota(jnp.int32, shape, dim)


def band_table():
    row, lane = iota((96, 128), 0), iota((96, 128), 1)
    return ((lane >> 2) == (row & 31) + (row >> 5) - 1).astype(F32).astype(BF)


def row_mask():
    return (iota((128, 128), 0) >> 5) == (iota((128, 128), 1) & 3)


def strips_kernel(src_ref, out_ref, wide, stage):
    wide[...] = src_ref[...].astype(F32)
    table = band_table()
    mask = row_mask()
    for x in range(8):
        own = wide[pl.ds(x, 160, stride=8), :]
        parts = []
        for v in range(VIEWS):
            part = own[v * 32 : (v + 1) * 32]
            parts.append(jnp.where(mask, jnp.concatenate([part] * 4, axis=0), 0.0).astype(BF))
        stacked = jnp.concatenate(parts, axis=0)
        moved = lax.dot_general(table, stacked, NT, preferred_element_type=F32)
        for v in range(VIEWS):
            for band in range(3):
                stage[v * 3 + band, pl.ds(x, 32, stride=8), :] = moved[
                    band * 32 : (band + 1) * 32, v * 128 : (v + 1) * 128
                ]
    for piece in range(VIEWS * 3):
        out_ref[:, piece * 128 : (piece + 1) * 128] = stage[piece].astype(BF)


def strips(source):
    return pl.pallas_call(
        strips_kernel,
        out_shape=jax.ShapeDtypeStruct((256, VIEWS * 384), BF),
        in_specs=[whole()],
        out_specs=whole(),
        scratch_shapes=[pltpu.VMEM((1280, 128), F32), pltpu.VMEM((VIEWS * 3, 256, 128), F32)],
        compiler_params=params(),
        name="strips",
    )(source)


def unstrips_kernel(in_ref, out_ref, wide):
    for piece in range(VIEWS * 3):
        wide[piece] = in_ref[:, piece * 128 : (piece + 1) * 128].astype(F32)
    table = band_table()
    mask = row_mask()
    for x in range(8):
        columns = []
        for v in range(VIEWS):
            bands = [wide[v * 3 + band, pl.ds(x, 32, stride=8), :] for band in range(3)]
            columns.append(jnp.concatenate(bands, axis=0).astype(BF))
        stacked = jnp.concatenate(columns, axis=1)
        moved = lax.dot_general(stacked, table, TN, preferred_element_type=F32)
        parts = []
        for v in range(VIEWS):
            part = jnp.where(mask, moved[v * 128 : (v + 1) * 128], 0.0)
            parts.append((part[0:32] + part[32:64]) + (part[64:96] + part[96:128]))
        out_ref[pl.ds(x, 160, stride=8), :] = jnp.concatenate(parts, axis=0)


def unstrips(arrived):
    return pl.pallas_call(
        unstrips_kernel,
        out_shape=jax.ShapeDtypeStruct((1280, 128), F32),
        in_specs=[whole()],
        out_specs=whole(),
        scratch_shapes=[pltpu.VMEM((VIEWS * 3, 256, 128), F32)],
        compiler_params=params(),
        name="unstrips",
    )(arrived)


def half_mask(rows):
    return iota((rows, 128), 1) < 64


def spread_interp(values):
    parts = []
    zero = jnp.zeros((64, 64), BF)
    for k in range(4):
        parts.append(jnp.concatenate([values[k], zero], axis=1))
        parts.append(jnp.concatenate([zero, values[k]], axis=1))
    return jnp.concatenate(parts, axis=0)


def pair_swap(low, high):
    mask = half_mask(low.shape[0])
    first = jnp.where(mask, low, pltpu.roll(high, 64, 1))
    second = jnp.where(mask, pltpu.roll(low, 64, 1), high)
    return first, second


def turn_kernel(in_ref, blocks_ref):
    for view in range(VIEWS):
        turned = in_ref[:, view * 384 : (view + 1) * 384].astype(F32).T
        for band_row in range(12):
            upper = turned[band_row * 32 : band_row * 32 + 16]
            lower = turned[band_row * 32 + 16 : band_row * 32 + 32]
            for half in range(2):
                even, odd = pair_swap(
                    upper[:, half * 128 : half * 128 + 128], lower[:, half * 128 : half * 128 + 128]
                )
                at = view * SEGS + band_row * 4 + half * 2
                blocks_ref[at] = even.astype(BF)
                blocks_ref[at + 1] = odd.astype(BF)


def warp_planes(group, place_ref, order_ref, blocks_ref, interp_ref, first_ref, second_ref, warped_ref):
    first_ref[...] = jnp.zeros_like(first_ref)
    second_ref[...] = jnp.zeros_like(second_ref)

    def step(view, unused):
        for e in range(4):
            plane = order_ref[group * 4 + e]
            base = (view * PLANES + plane) * 64
            rows = []
            for g in range(16):
                taps = [blocks_ref[view * SEGS + place_ref[base + g * 4 + k]] for k in range(4)]
                rows.append(jnp.concatenate(taps, axis=1))
            picked = jnp.concatenate(rows, axis=0)
            matrix = spread_interp(interp_ref[view, plane])
            warped = lax.dot_general(picked, matrix, NN, preferred_element_type=F32)
            first_ref[e] += warped
            second_ref[e] += warped * warped
            warped_ref[view, e] = warped.astype(BF)
        return unused

    lax.fori_loop(0, VIEWS, step, 0, unroll=UNROLL)


def warp_other_kernel(
    place_ref, order_ref, in_ref, interp_ref, blocks_ref, first_ref, second_ref, warped_ref
):
    turn_kernel(in_ref, blocks_ref)
    warp_planes(0, place_ref, order_ref, blocks_ref, interp_ref, first_ref, second_ref, warped_ref)


def warp_mine_kernel(
    place_ref, order_ref, blocks_ref, interp_ref, first_ref, second_ref, warped_ref
):
    warp_planes(1, place_ref, order_ref, blocks_ref, interp_ref, first_ref, second_ref, warped_ref)


UNROLL = 5
SUMS = jax.ShapeDtypeStruct((4, 256, 128), F32)
WARPED = jax.ShapeDtypeStruct((VIEWS, 4, 256, 128), BF)
BLOCKS = jax.ShapeDtypeStruct((VIEWS * SEGS, 16, 128), BF)


def smem():
    return pl.BlockSpec(memory_space=pltpu.SMEM)


def warp_other(place, order, arrived, interp):
    return pl.pallas_call(
        warp_other_kernel,
        in_specs=[smem(), smem(), whole(), whole()],
        out_specs=[whole()] * 4,
        out_shape=[BLOCKS, SUMS, SUMS, WARPED],
        compiler_params=params(),
        name="warp_other",
    )(place, order, arrived, interp)


def warp_mine(place, order, blocks, interp):
    return pl.pallas_call(
        warp_mine_kernel,
        in_specs=[smem(), smem(), whole(), whole()],
        out_specs=[whole()] * 3,
        out_shape=[SUMS, SUMS, WARPED],
        compiler_params=params(),
        name="warp_mine",
    )(place, order, blocks, interp)


CHAINS = 4


def land_views(
    views, place_ref, order_ref, warped_o, warped_m, interp_ref, mean_o, mean_m, grad_ref, out_ref, accs
):
    groups = ((warped_o, mean_o), (warped_m, mean_m))
    for view in views:
        for acc in accs:
            acc[...] = jnp.zeros_like(acc)
        for e in range(8):
            warped_ref, mean_ref = groups[e // 4]
            plane = order_ref[e]
            base = (view * PLANES + plane) * 64
            warped = warped_ref[view, e % 4].astype(F32)
            grad = (grad_ref[plane] * (warped - mean_ref[e % 4].astype(F32))).astype(BF)
            matrix = spread_interp(interp_ref[view, plane])
            spread = lax.dot_general(grad, matrix, NT, preferred_element_type=F32)
            for g in range(16):
                for k in range(4):
                    where = place_ref[base + g * 4 + k]
                    accs[k][where] += spread[g * 16 : (g + 1) * 16, k * 128 : (k + 1) * 128]
        bands = []
        for band_row in range(12):
            columns_up, columns_low = [], []
            for half in range(2):
                at = band_row * 4 + half * 2
                even = (accs[0][at] + accs[1][at]) + (accs[2][at] + accs[3][at])
                odd = (accs[0][at + 1] + accs[1][at + 1]) + (accs[2][at + 1] + accs[3][at + 1])
                up, low = pair_swap(even, odd)
                columns_up.append(up)
                columns_low.append(low)
            bands.append(jnp.concatenate(columns_up, axis=1))
            bands.append(jnp.concatenate(columns_low, axis=1))
        out_ref[:, view * 384 : (view + 1) * 384] = jnp.concatenate(bands, axis=0).T.astype(BF)


def land_first_kernel(views, *refs):
    land_views(views, *refs[:9], refs[9:])


def land_next_kernel(views, *refs):
    land_views(views, *refs[:8], refs[9], refs[10:])


LANDED = jax.ShapeDtypeStruct((256, VIEWS * 384), BF)


def land(views, place, order, warped_o, warped_m, interp, mean_o, mean_m, grad, earlier=None):
    operands = [place, order, warped_o, warped_m, interp, mean_o, mean_m, grad]
    specs = [smem(), smem()] + [whole()] * 6
    if earlier is None:
        kernel, aliases = land_first_kernel, {}
    else:
        kernel, aliases = land_next_kernel, {8: 0}
        operands.append(earlier)
        specs.append(whole())
    return pl.pallas_call(
        functools.partial(kernel, views),
        in_specs=specs,
        out_specs=whole(),
        out_shape=LANDED,
        scratch_shapes=[pltpu.VMEM((SEGS, 16, 128), F32)] * CHAINS,
        input_output_aliases=aliases,
        compiler_params=params(),
        cost_estimate=SMALL,
        name="land",
    )(*operands)


def chip_first_kernel(mine_ref, arrived_ref, sum_ref, send_ref):
    total = mine_ref[...] + arrived_ref[...]
    sum_ref[...] = total
    send_ref[...] = total.astype(BF)


def chip_second_kernel(where_ref, mine_ref, arrived_ref, own_ref, send_ref):
    core = where_ref[1]
    own_ref[0:2] = mine_ref[2:4] + arrived_ref[2:4]
    own_ref[2] = mine_ref[core] + arrived_ref[core]
    send_ref[0:2] = mine_ref[0:2] + arrived_ref[0:2]
    send_ref[2] = mine_ref[2 + core] + arrived_ref[2 + core]


def chip_first(mine, arrived):
    return pl.pallas_call(
        chip_first_kernel,
        in_specs=[whole()] * 2,
        out_specs=[whole()] * 2,
        out_shape=[SUMS, jax.ShapeDtypeStruct(SUMS.shape, BF)],
        compiler_params=params(),
        name="chip_first",
    )(mine, arrived)


def chip_second(where, mine, arrived):
    return pl.pallas_call(
        chip_second_kernel,
        in_specs=[smem()] + [whole()] * 2,
        out_specs=[whole()] * 2,
        out_shape=[jax.ShapeDtypeStruct((3, 256, 128), F32)] * 2,
        compiler_params=params(),
        name="chip_second",
    )(where, mine, arrived)


def turned_reference(ref_ref, pair):
    lanes = slice(pair * 128, pair * 128 + 128)
    even, odd = pair_swap(ref_ref[0:16, lanes].astype(F32), ref_ref[16:32, lanes].astype(F32))
    return jnp.concatenate([even, odd], axis=0)


def mean_kernel(sum_ref, there_ref, ref_ref, mean_ref):
    for pair in range(8):
        rows = slice(pair * 32, pair * 32 + 32)
        ref = turned_reference(ref_ref, pair)
        for e in range(4):
            total = sum_ref[e, rows] + there_ref[e ^ 2, rows].astype(F32) + ref
            mean_ref[e, rows] = (total * (1.0 / COUNT)).astype(BF)


def mean_of(sums, there, reference):
    return pl.pallas_call(
        mean_kernel,
        in_specs=[whole()] * 3,
        out_specs=whole(),
        out_shape=jax.ShapeDtypeStruct(SUMS.shape, BF),
        compiler_params=params(),
        name="mean",
    )(sums, there, reference)


def cost_kernel(
    where_ref, first_ref, first_there, second_ref, second_there, ref_ref, low_ref, high_ref, send_ref
):
    y_low, core = where_ref[0], where_ref[1]
    inside = jnp.where(y_low == core, 1.0, 0.0)
    for pair in range(8):
        rows = slice(pair * 32, pair * 32 + 32)
        ref = turned_reference(ref_ref, pair)
        square = ref * ref

        def plane_cost(mine, there, slot):
            first = first_ref[mine, rows] + first_there[there, rows].astype(F32) + ref
            second = second_ref[slot, rows] + second_there[slot, rows] + square
            mean = first * (1.0 / COUNT)
            return second * (1.0 / COUNT) - mean * mean

        low = plane_cost(2, 0, 0)
        high = plane_cost(3, 1, 1)
        far = plane_cost(core, 2 + core, 2)
        low_ref[0, rows] = low.astype(BF)
        high_ref[0, rows] = high.astype(BF)
        send_ref[0, rows] = jnp.where(core == 1, low, high).astype(BF)
        send_ref[1, rows] = (far * inside).astype(BF)


def edges_kernel(where_ref, low_ref, high_ref, near_ref, outer_ref, last_ref, initial_ref):
    core = where_ref[1]
    outer_ref[0] = near_ref[1 - core]
    outer_ref[1] = near_ref[core]
    for local, plane in ((0, outer_ref[0]), (1, low_ref[0]), (2, high_ref[0]), (3, outer_ref[1])):
        last_ref[local] = plane[192:256]
        initial_ref[local] = plane[0:64]


PLANE = jax.ShapeDtypeStruct((1, 256, 128), BF)
PAIR = jax.ShapeDtypeStruct((2, 256, 128), BF)
EDGES = jax.ShapeDtypeStruct((4, 64, 128), BF)


def cost_of(where, first, first_there, second, second_there, reference):
    return pl.pallas_call(
        cost_kernel,
        in_specs=[smem()] + [whole()] * 5,
        out_specs=[whole()] * 3,
        out_shape=[PLANE, PLANE, PAIR],
        compiler_params=params(),
        name="cost",
    )(where, first, first_there, second, second_there, reference)


def edges_of(where, low, high, near):
    return pl.pallas_call(
        edges_kernel,
        in_specs=[smem()] + [whole()] * 3,
        out_specs=[whole()] * 3,
        out_shape=[PAIR, EDGES, EDGES],
        compiler_params=params(),
        name="edges",
    )(where, low, high, near)


def slots_kernel(*refs):
    for slot in range(4):
        refs[4][slot] = refs[slot][...]
        refs[5][slot] = refs[slot][:, :, 768:1024]
        refs[6][slot] = refs[slot][:, :, 0:256]


def slots_of(parts):
    row = jax.ShapeDtypeStruct((4, 2, 8, 256), BF)
    return pl.pallas_call(
        slots_kernel,
        in_specs=[whole()] * 4,
        out_specs=[whole()] * 3,
        out_shape=[jax.ShapeDtypeStruct((4, 2, 8, 1024), BF), row, row],
        compiler_params=params(),
        name="slots",
    )(*parts)


def shifted(values, offset):
    lanes = values.shape[1]
    col = iota(values.shape, 1) & 255
    if offset > 0:
        return jnp.where(col == 255, 0.0, pltpu.roll(values, lanes - 1, 1))
    return jnp.where(col == 0, 0.0, pltpu.roll(values, 1, 1))


def grad_cost_kernel(view_ref, own_ref, top_ref, bottom_ref, weight_ref, out_ref):
    view = view_ref[0]
    padded = []
    for plane in range(PLANES):
        slot = jnp.bitwise_xor(view, plane // 2)
        line = jnp.concatenate(
            [
                top_ref[slot, plane % 2].astype(F32),
                own_ref[slot, plane % 2].astype(F32),
                bottom_ref[slot, plane % 2].astype(F32),
            ],
            axis=1,
        )
        padded.append(jnp.concatenate([shifted(line, 1), line, shifted(line, -1)], axis=0))
    zero = jnp.zeros_like(padded[0])
    weight = weight_ref[...]
    for plane in range(PLANES):
        near = [padded[p] if 0 <= p < PLANES else zero for p in (plane + 1, plane, plane - 1)]
        result = lax.dot_general(
            weight, jnp.concatenate(near, axis=0).astype(BF), NN, preferred_element_type=F32
        )
        grad = result[0:32, 512:1536] + result[32:64, 256:1280] + result[64:96, 0:1024]
        grad = grad * (2.0 / COUNT)
        for pair in range(8):
            upper = grad[0:16, pair * 128 : pair * 128 + 128]
            lower = grad[16:32, pair * 128 : pair * 128 + 128]
            even, odd = pair_swap(upper, lower)
            out_ref[plane, pair * 32 : pair * 32 + 16] = even
            out_ref[plane, pair * 32 + 16 : pair * 32 + 32] = odd


def grad_cost(view, own, top, bottom, weight):
    return pl.pallas_call(
        grad_cost_kernel,
        out_shape=jax.ShapeDtypeStruct((PLANES, 256, 128), F32),
        in_specs=[pl.BlockSpec(memory_space=pltpu.SMEM)] + [whole()] * 4,
        out_specs=whole(),
        compiler_params=params(),
        name="grad_cost",
    )(view, own, top, bottom, weight)


def conv_kernel(outer_ref, low_ref, high_ref, top_ref, bottom_ref, weight_ref, out_ref):
    weight = weight_ref[...]
    results = []
    for local in range(4):
        middle = (outer_ref, low_ref, high_ref, outer_ref)[local][1 if local == 3 else 0]
        tall = jnp.concatenate([top_ref[local], middle, bottom_ref[local]], axis=0).astype(F32)
        upper, lower = [], []
        for pair in range(12):
            even = tall[pair * 32 : pair * 32 + 16]
            odd = tall[pair * 32 + 16 : pair * 32 + 32]
            up, low = pair_swap(even, odd)
            upper.append(up)
            lower.append(low)
        line = jnp.concatenate(
            [jnp.concatenate(upper, axis=1), jnp.concatenate(lower, axis=1)], axis=0
        )
        wide = jnp.concatenate([shifted(line, -1), line, shifted(line, 1)], axis=0).astype(BF)
        results.append(lax.dot_general(weight, wide, NN, preferred_element_type=F32))
    for plane in range(2):
        total = None
        for a in range(3):
            for b in range(3):
                at = (a * 3 + b) * 8
                part = results[plane + a][at : at + 8, b * 256 : b * 256 + 1024]
                total = part if total is None else total + part
        out_ref[plane] = total.astype(BF)


def conv(outer, low, high, top, bottom, weight):
    return pl.pallas_call(
        conv_kernel,
        out_shape=jax.ShapeDtypeStruct((2, 8, 1024), BF),
        in_specs=[whole()] * 6,
        out_specs=whole(),
        compiler_params=params(),
        name="conv",
    )(outer, low, high, top, bottom, weight)


def body(
    source_features,
    reference_features,
    interp,
    source_tile,
    source_block,
    conv_weight,
    grad_regularized,
):
    tiles = lax.axis_size("tile")
    views = lax.axis_size("view")
    view = lax.axis_index("view")
    up = [(i, i + 1) for i in range(tiles - 1)]
    down = [(i + 1, i) for i in range(tiles - 1)]

    def other(array, mask):
        return lax.ppermute(array, "view", [(i, i ^ mask) for i in range(views)])

    slots = jnp.arange(8, dtype=jnp.int32)
    y_low, core = view // 2, view % 2
    order = (
        ((slots // 2) % 2 ^ 1 ^ y_low) * 4 + ((slots // 4) ^ 1 ^ core) * 2 + slots % 2
    ).astype(jnp.int32)
    place = ((source_tile + 1) * 16 + source_block).reshape(-1)

    where = jnp.stack([y_low, core]).astype(jnp.int32)
    own = grad_regularized
    parts = (own, other(own, 1), other(own, 2), other(own, 3))
    operand = strips(source_features.reshape(1280, 128))
    cotangent, last, initial = slots_of(parts)
    operand, last, initial = lax.optimization_barrier((operand, last, initial))
    arrived = lax.all_to_all(operand, "tile", split_axis=0, concat_axis=0, tiled=True)
    top = lax.ppermute(last, "tile", up)
    bottom = lax.ppermute(initial, "tile", down)
    back_weight = conv_weight.transpose(1, 4, 0, 2, 3).reshape(96, 72)
    weight = conv_weight.transpose(0, 1, 3, 2, 4).reshape(72, 96)
    grad = grad_cost(view.astype(jnp.int32).reshape(1), cotangent, top, bottom, back_weight)
    arrived, grad, weight = lax.optimization_barrier((arrived, grad, weight))

    blocks, first_o, second_o, warped_o = warp_other(place, order, arrived, interp)
    first_m, second_m, warped_m = warp_mine(place, order, blocks, interp)
    first_chip, first_send = chip_first(first_m, other(first_o, 1))
    first_there = other(first_send, 2)
    second_own, second_send = chip_second(where, second_m, other(second_o, 1))
    second_there = other(second_send, 2)
    first_there, second_own = lax.optimization_barrier((first_there, second_own))
    mean_mine = mean_of(first_chip, first_there, reference_features)
    mean_other = other(mean_mine, 1)

    shared = (place, order, warped_o, warped_m, interp, mean_other, mean_mine, grad)
    landed = land((0, 1, 2), *shared)
    landed, second_there = lax.optimization_barrier((landed, second_there))
    low, high, send = cost_of(
        where, first_chip, first_there, second_own, second_there, reference_features
    )
    near = other(send, 1)
    landed = land((3, 4), *shared, landed)
    landed, near = lax.optimization_barrier((landed, near))
    outer, cost_last, cost_initial = edges_of(where, low, high, near)
    landed, cost_last, cost_initial = lax.optimization_barrier((landed, cost_last, cost_initial))
    returned = lax.all_to_all(landed, "tile", split_axis=0, concat_axis=0, tiled=True)
    cost_top = lax.ppermute(cost_last, "tile", up)
    cost_bottom = lax.ppermute(cost_initial, "tile", down)
    regularized = conv(outer, low, high, cost_top, cost_bottom, weight)

    grad_source = unstrips(returned).reshape(source_features.shape)
    return regularized, grad_source


def solution(mesh):
    return jax.shard_map(
        body,
        mesh=mesh,
        in_specs=(
            P("view", None, "tile", None),
            P(None, "tile"),
            P("view", None, None, None, None),
            P("view", None, "tile", None),
            P("view", None, "tile", None),
            P(),
            P("view", None, "tile"),
        ),
        out_specs=(P("view", None, "tile"), P("view", None, "tile", None)),
        check_vma=False,
    )
```

```python
import functools

import jax
import jax.numpy as jnp
from jax import lax
from jax.experimental import pallas as pl
from jax.experimental.pallas import tpu as pltpu
from jax.sharding import PartitionSpec as P

BF = jnp.bfloat16
F32 = jnp.float32
VIEWS = 5
PLANES = 8
COUNT = 21.0
SEGS = 48
VMEM_LIMIT = 4 * 1024 * 1024
NT = (((1,), (1,)), ((), ()))
NN = (((1,), (0,)), ((), ()))
TN = (((0,), (0,)), ((), ()))


def params():
    return pltpu.CompilerParams(vmem_limit_bytes=VMEM_LIMIT)


def whole():
    return pl.BlockSpec(memory_space=pltpu.VMEM)


SMALL = pl.CostEstimate(flops=1000, bytes_accessed=1000, transcendentals=0)


def iota(shape, dim):
    return lax.broadcasted_iota(jnp.int32, shape, dim)


def band_table():
    row, lane = iota((96, 128), 0), iota((96, 128), 1)
    return ((lane >> 2) == (row & 31) + (row >> 5) - 1).astype(F32).astype(BF)


def row_mask():
    return (iota((128, 128), 0) >> 5) == (iota((128, 128), 1) & 3)


def strips_kernel(src_ref, out_ref, wide, stage):
    wide[...] = src_ref[...].astype(F32)
    table = band_table()
    mask = row_mask()
    for x in range(8):
        own = wide[pl.ds(x, 160, stride=8), :]
        parts = []
        for v in range(VIEWS):
            part = own[v * 32 : (v + 1) * 32]
            parts.append(jnp.where(mask, jnp.concatenate([part] * 4, axis=0), 0.0).astype(BF))
        stacked = jnp.concatenate(parts, axis=0)
        moved = lax.dot_general(table, stacked, NT, preferred_element_type=F32)
        for v in range(VIEWS):
            for band in range(3):
                stage[v * 3 + band, pl.ds(x, 32, stride=8), :] = moved[
                    band * 32 : (band + 1) * 32, v * 128 : (v + 1) * 128
                ]
    for piece in range(VIEWS * 3):
        out_ref[:, piece * 128 : (piece + 1) * 128] = stage[piece].astype(BF)


def strips(source):
    return pl.pallas_call(
        strips_kernel,
        out_shape=jax.ShapeDtypeStruct((256, VIEWS * 384), BF),
        in_specs=[whole()],
        out_specs=whole(),
        scratch_shapes=[pltpu.VMEM((1280, 128), F32), pltpu.VMEM((VIEWS * 3, 256, 128), F32)],
        compiler_params=params(),
        name="strips",
    )(source)


def unstrips_kernel(in_ref, out_ref, wide):
    for piece in range(VIEWS * 3):
        wide[piece] = in_ref[:, piece * 128 : (piece + 1) * 128].astype(F32)
    table = band_table()
    mask = row_mask()
    for x in range(8):
        columns = []
        for v in range(VIEWS):
            bands = [wide[v * 3 + band, pl.ds(x, 32, stride=8), :] for band in range(3)]
            columns.append(jnp.concatenate(bands, axis=0).astype(BF))
        stacked = jnp.concatenate(columns, axis=1)
        moved = lax.dot_general(stacked, table, TN, preferred_element_type=F32)
        parts = []
        for v in range(VIEWS):
            part = jnp.where(mask, moved[v * 128 : (v + 1) * 128], 0.0)
            parts.append((part[0:32] + part[32:64]) + (part[64:96] + part[96:128]))
        out_ref[pl.ds(x, 160, stride=8), :] = jnp.concatenate(parts, axis=0)


def unstrips(arrived):
    return pl.pallas_call(
        unstrips_kernel,
        out_shape=jax.ShapeDtypeStruct((1280, 128), F32),
        in_specs=[whole()],
        out_specs=whole(),
        scratch_shapes=[pltpu.VMEM((VIEWS * 3, 256, 128), F32)],
        compiler_params=params(),
        name="unstrips",
    )(arrived)


def half_mask(rows):
    return iota((rows, 128), 1) < 64


def spread_interp(values):
    parts = []
    zero = jnp.zeros((64, 64), BF)
    for k in range(4):
        parts.append(jnp.concatenate([values[k], zero], axis=1))
        parts.append(jnp.concatenate([zero, values[k]], axis=1))
    return jnp.concatenate(parts, axis=0)


def pair_swap(low, high):
    mask = half_mask(low.shape[0])
    first = jnp.where(mask, low, pltpu.roll(high, 64, 1))
    second = jnp.where(mask, pltpu.roll(low, 64, 1), high)
    return first, second


def turn_kernel(in_ref, blocks_ref):
    for view in range(VIEWS):
        turned = in_ref[:, view * 384 : (view + 1) * 384].astype(F32).T
        for band_row in range(12):
            upper = turned[band_row * 32 : band_row * 32 + 16]
            lower = turned[band_row * 32 + 16 : band_row * 32 + 32]
            for half in range(2):
                even, odd = pair_swap(
                    upper[:, half * 128 : half * 128 + 128], lower[:, half * 128 : half * 128 + 128]
                )
                at = view * SEGS + band_row * 4 + half * 2
                blocks_ref[at] = even.astype(BF)
                blocks_ref[at + 1] = odd.astype(BF)


def warp_planes(group, place_ref, order_ref, blocks_ref, interp_ref, first_ref, second_ref, warped_ref):
    first_ref[...] = jnp.zeros_like(first_ref)
    second_ref[...] = jnp.zeros_like(second_ref)

    def step(view, unused):
        for e in range(4):
            plane = order_ref[group * 4 + e]
            base = (view * PLANES + plane) * 64
            rows = []
            for g in range(16):
                taps = [blocks_ref[view * SEGS + place_ref[base + g * 4 + k]] for k in range(4)]
                rows.append(jnp.concatenate(taps, axis=1))
            picked = jnp.concatenate(rows, axis=0)
            matrix = spread_interp(interp_ref[view, plane])
            warped = lax.dot_general(picked, matrix, NN, preferred_element_type=F32)
            first_ref[e] += warped
            second_ref[e] += warped * warped
            warped_ref[view, e] = warped.astype(BF)
        return unused

    lax.fori_loop(0, VIEWS, step, 0, unroll=UNROLL)


def warp_other_kernel(
    place_ref, order_ref, in_ref, interp_ref, blocks_ref, first_ref, second_ref, warped_ref
):
    turn_kernel(in_ref, blocks_ref)
    warp_planes(0, place_ref, order_ref, blocks_ref, interp_ref, first_ref, second_ref, warped_ref)


def warp_mine_kernel(
    place_ref, order_ref, blocks_ref, interp_ref, first_ref, second_ref, warped_ref
):
    warp_planes(1, place_ref, order_ref, blocks_ref, interp_ref, first_ref, second_ref, warped_ref)


UNROLL = 5
SUMS = jax.ShapeDtypeStruct((4, 256, 128), F32)
WARPED = jax.ShapeDtypeStruct((VIEWS, 4, 256, 128), BF)
BLOCKS = jax.ShapeDtypeStruct((VIEWS * SEGS, 16, 128), BF)


def smem():
    return pl.BlockSpec(memory_space=pltpu.SMEM)


def warp_other(place, order, arrived, interp):
    return pl.pallas_call(
        warp_other_kernel,
        in_specs=[smem(), smem(), whole(), whole()],
        out_specs=[whole()] * 4,
        out_shape=[BLOCKS, SUMS, SUMS, WARPED],
        compiler_params=params(),
        name="warp_other",
    )(place, order, arrived, interp)


def warp_mine(place, order, blocks, interp):
    return pl.pallas_call(
        warp_mine_kernel,
        in_specs=[smem(), smem(), whole(), whole()],
        out_specs=[whole()] * 3,
        out_shape=[SUMS, SUMS, WARPED],
        compiler_params=params(),
        name="warp_mine",
    )(place, order, blocks, interp)


CHAINS = 4


def land_views(
    views, place_ref, order_ref, warped_o, warped_m, interp_ref, mean_o, mean_m, grad_ref, out_ref, accs
):
    groups = ((warped_o, mean_o), (warped_m, mean_m))
    for view in views:
        for acc in accs:
            acc[...] = jnp.zeros_like(acc)
        for e in range(8):
            warped_ref, mean_ref = groups[e // 4]
            plane = order_ref[e]
            base = (view * PLANES + plane) * 64
            warped = warped_ref[view, e % 4].astype(F32)
            grad = (grad_ref[plane] * (warped - mean_ref[e % 4].astype(F32))).astype(BF)
            matrix = spread_interp(interp_ref[view, plane])
            spread = lax.dot_general(grad, matrix, NT, preferred_element_type=F32)
            for g in range(16):
                for k in range(4):
                    where = place_ref[base + g * 4 + k]
                    accs[k][where] += spread[g * 16 : (g + 1) * 16, k * 128 : (k + 1) * 128]
        bands = []
        for band_row in range(12):
            columns_up, columns_low = [], []
            for half in range(2):
                at = band_row * 4 + half * 2
                even = (accs[0][at] + accs[1][at]) + (accs[2][at] + accs[3][at])
                odd = (accs[0][at + 1] + accs[1][at + 1]) + (accs[2][at + 1] + accs[3][at + 1])
                up, low = pair_swap(even, odd)
                columns_up.append(up)
                columns_low.append(low)
            bands.append(jnp.concatenate(columns_up, axis=1))
            bands.append(jnp.concatenate(columns_low, axis=1))
        lane = (view - views[0]) * 384
        out_ref[:, lane : lane + 384] = jnp.concatenate(bands, axis=0).T.astype(BF)


def land_first_kernel(views, *refs):
    land_views(views, *refs[:9], refs[9:])


def land_last_kernel(views, *refs):
    earlier_ref, out_hbm, own_ref, sem = refs[8], refs[9], refs[10], refs[11]
    lanes = earlier_ref.shape[1]
    first = pltpu.make_async_copy(earlier_ref, out_hbm.at[:, 0:lanes], sem.at[0])
    first.start()
    land_views(views, *refs[:8], own_ref, refs[12:])
    last = pltpu.make_async_copy(own_ref, out_hbm.at[:, lanes : VIEWS * 384], sem.at[1])
    last.start()
    first.wait()
    last.wait()


ACCUMULATORS = [pltpu.VMEM((SEGS, 16, 128), F32)] * CHAINS


def land_first(views, *operands):
    return pl.pallas_call(
        functools.partial(land_first_kernel, views),
        in_specs=[smem(), smem()] + [whole()] * 6,
        out_specs=whole(),
        out_shape=jax.ShapeDtypeStruct((256, len(views) * 384), BF),
        scratch_shapes=ACCUMULATORS,
        compiler_params=params(),
        cost_estimate=SMALL,
        name="land_first",
    )(*operands)


def land_last(views, *operands):
    return pl.pallas_call(
        functools.partial(land_last_kernel, views),
        in_specs=[smem(), smem()] + [whole()] * 7,
        out_specs=pl.BlockSpec(memory_space=pltpu.HBM),
        out_shape=pltpu.HBM((256, VIEWS * 384), BF),
        scratch_shapes=[
            pltpu.VMEM((256, len(views) * 384), BF),
            pltpu.SemaphoreType.DMA((2,)),
        ]
        + ACCUMULATORS,
        compiler_params=params(),
        cost_estimate=SMALL,
        name="land_last",
    )(*operands)


def chip_first_kernel(mine_ref, arrived_ref, sum_ref, send_ref):
    total = mine_ref[...] + arrived_ref[...]
    sum_ref[...] = total
    send_ref[...] = total.astype(BF)


def chip_second_kernel(where_ref, mine_ref, arrived_ref, own_ref, send_ref):
    core = where_ref[1]
    own_ref[0:2] = mine_ref[2:4] + arrived_ref[2:4]
    own_ref[2] = mine_ref[core] + arrived_ref[core]
    send_ref[0:2] = mine_ref[0:2] + arrived_ref[0:2]
    send_ref[2] = mine_ref[2 + core] + arrived_ref[2 + core]


def chip_first(mine, arrived):
    return pl.pallas_call(
        chip_first_kernel,
        in_specs=[whole()] * 2,
        out_specs=[whole()] * 2,
        out_shape=[SUMS, jax.ShapeDtypeStruct(SUMS.shape, BF)],
        compiler_params=params(),
        name="chip_first",
    )(mine, arrived)


def chip_second(where, mine, arrived):
    return pl.pallas_call(
        chip_second_kernel,
        in_specs=[smem()] + [whole()] * 2,
        out_specs=[whole()] * 2,
        out_shape=[jax.ShapeDtypeStruct((3, 256, 128), F32)] * 2,
        compiler_params=params(),
        name="chip_second",
    )(where, mine, arrived)


def turned_reference(ref_ref, pair):
    lanes = slice(pair * 128, pair * 128 + 128)
    even, odd = pair_swap(ref_ref[0:16, lanes].astype(F32), ref_ref[16:32, lanes].astype(F32))
    return jnp.concatenate([even, odd], axis=0)


def mean_kernel(sum_ref, there_ref, ref_ref, mean_ref):
    for pair in range(8):
        rows = slice(pair * 32, pair * 32 + 32)
        ref = turned_reference(ref_ref, pair)
        for e in range(4):
            total = sum_ref[e, rows] + there_ref[e ^ 2, rows].astype(F32) + ref
            mean_ref[e, rows] = (total * (1.0 / COUNT)).astype(BF)


def mean_of(sums, there, reference):
    return pl.pallas_call(
        mean_kernel,
        in_specs=[whole()] * 3,
        out_specs=whole(),
        out_shape=jax.ShapeDtypeStruct(SUMS.shape, BF),
        compiler_params=params(),
        name="mean",
    )(sums, there, reference)


def cost_kernel(
    where_ref, first_ref, first_there, second_ref, second_there, ref_ref, low_ref, high_ref, send_ref
):
    y_low, core = where_ref[0], where_ref[1]
    inside = jnp.where(y_low == core, 1.0, 0.0)
    for pair in range(8):
        rows = slice(pair * 32, pair * 32 + 32)
        ref = turned_reference(ref_ref, pair)
        square = ref * ref

        def plane_cost(mine, there, slot):
            first = first_ref[mine, rows] + first_there[there, rows].astype(F32) + ref
            second = second_ref[slot, rows] + second_there[slot, rows] + square
            mean = first * (1.0 / COUNT)
            return second * (1.0 / COUNT) - mean * mean

        low = plane_cost(2, 0, 0)
        high = plane_cost(3, 1, 1)
        far = plane_cost(core, 2 + core, 2)
        low_ref[0, rows] = low.astype(BF)
        high_ref[0, rows] = high.astype(BF)
        send_ref[0, rows] = jnp.where(core == 1, low, high).astype(BF)
        send_ref[1, rows] = (far * inside).astype(BF)


def edges_kernel(where_ref, low_ref, high_ref, near_ref, outer_ref, last_ref, initial_ref):
    core = where_ref[1]
    outer_ref[0] = near_ref[1 - core]
    outer_ref[1] = near_ref[core]
    for local, plane in ((0, outer_ref[0]), (1, low_ref[0]), (2, high_ref[0]), (3, outer_ref[1])):
        last_ref[local] = plane[192:256]
        initial_ref[local] = plane[0:64]


PLANE = jax.ShapeDtypeStruct((1, 256, 128), BF)
PAIR = jax.ShapeDtypeStruct((2, 256, 128), BF)
EDGES = jax.ShapeDtypeStruct((4, 64, 128), BF)


def cost_of(where, first, first_there, second, second_there, reference):
    return pl.pallas_call(
        cost_kernel,
        in_specs=[smem()] + [whole()] * 5,
        out_specs=[whole()] * 3,
        out_shape=[PLANE, PLANE, PAIR],
        compiler_params=params(),
        name="cost",
    )(where, first, first_there, second, second_there, reference)


def edges_of(where, low, high, near):
    return pl.pallas_call(
        edges_kernel,
        in_specs=[smem()] + [whole()] * 3,
        out_specs=[whole()] * 3,
        out_shape=[PAIR, EDGES, EDGES],
        compiler_params=params(),
        name="edges",
    )(where, low, high, near)


def slots_kernel(*refs):
    for slot in range(4):
        refs[4][slot] = refs[slot][...]
        refs[5][slot] = refs[slot][:, :, 768:1024]
        refs[6][slot] = refs[slot][:, :, 0:256]


def slots_of(parts):
    row = jax.ShapeDtypeStruct((4, 2, 8, 256), BF)
    return pl.pallas_call(
        slots_kernel,
        in_specs=[whole()] * 4,
        out_specs=[whole()] * 3,
        out_shape=[jax.ShapeDtypeStruct((4, 2, 8, 1024), BF), row, row],
        compiler_params=params(),
        name="slots",
    )(*parts)


def shifted(values, offset):
    lanes = values.shape[1]
    col = iota(values.shape, 1) & 255
    if offset > 0:
        return jnp.where(col == 255, 0.0, pltpu.roll(values, lanes - 1, 1))
    return jnp.where(col == 0, 0.0, pltpu.roll(values, 1, 1))


def grad_cost_kernel(
    view_ref, own_ref, top_ref, bottom_ref, weight_ref, out_hbm, out_ref, sem
):
    view = view_ref[0]
    padded = []
    for plane in range(PLANES):
        slot = jnp.bitwise_xor(view, plane // 2)
        line = jnp.concatenate(
            [
                top_ref[slot, plane % 2].astype(F32),
                own_ref[slot, plane % 2].astype(F32),
                bottom_ref[slot, plane % 2].astype(F32),
            ],
            axis=1,
        )
        padded.append(jnp.concatenate([shifted(line, 1), line, shifted(line, -1)], axis=0))
    zero = jnp.zeros_like(padded[0])
    weight = weight_ref[...]
    stores = []
    for plane in range(PLANES):
        near = [padded[p] if 0 <= p < PLANES else zero for p in (plane + 1, plane, plane - 1)]
        result = lax.dot_general(
            weight, jnp.concatenate(near, axis=0).astype(BF), NN, preferred_element_type=F32
        )
        grad = result[0:32, 512:1536] + result[32:64, 256:1280] + result[64:96, 0:1024]
        grad = grad * (2.0 / COUNT)
        for pair in range(8):
            upper = grad[0:16, pair * 128 : pair * 128 + 128]
            lower = grad[16:32, pair * 128 : pair * 128 + 128]
            even, odd = pair_swap(upper, lower)
            out_ref[plane, pair * 32 : pair * 32 + 16] = even
            out_ref[plane, pair * 32 + 16 : pair * 32 + 32] = odd
        if plane % 4 == 3:
            part = pl.ds(plane - 3, 4)
            stores.append(
                pltpu.make_async_copy(out_ref.at[part], out_hbm.at[part], sem.at[plane // 4])
            )
            stores[-1].start()
    for store in stores:
        store.wait()


def grad_cost(view, own, top, bottom, weight):
    return pl.pallas_call(
        grad_cost_kernel,
        out_shape=pltpu.HBM((PLANES, 256, 128), F32),
        in_specs=[pl.BlockSpec(memory_space=pltpu.SMEM)] + [whole()] * 4,
        out_specs=pl.BlockSpec(memory_space=pltpu.HBM),
        scratch_shapes=[pltpu.VMEM((PLANES, 256, 128), F32), pltpu.SemaphoreType.DMA((2,))],
        compiler_params=params(),
        name="grad_cost",
    )(view, own, top, bottom, weight)


def conv_kernel(outer_ref, low_ref, high_ref, top_ref, bottom_ref, weight_ref, out_ref):
    weight = weight_ref[...]
    results = []
    for local in range(4):
        middle = (outer_ref, low_ref, high_ref, outer_ref)[local][1 if local == 3 else 0]
        tall = jnp.concatenate([top_ref[local], middle, bottom_ref[local]], axis=0).astype(F32)
        upper, lower = [], []
        for pair in range(12):
            even = tall[pair * 32 : pair * 32 + 16]
            odd = tall[pair * 32 + 16 : pair * 32 + 32]
            up, low = pair_swap(even, odd)
            upper.append(up)
            lower.append(low)
        line = jnp.concatenate(
            [jnp.concatenate(upper, axis=1), jnp.concatenate(lower, axis=1)], axis=0
        )
        wide = jnp.concatenate([shifted(line, -1), line, shifted(line, 1)], axis=0).astype(BF)
        results.append(lax.dot_general(weight, wide, NN, preferred_element_type=F32))
    for plane in range(2):
        total = None
        for a in range(3):
            for b in range(3):
                at = (a * 3 + b) * 8
                part = results[plane + a][at : at + 8, b * 256 : b * 256 + 1024]
                total = part if total is None else total + part
        out_ref[plane] = total.astype(BF)


def conv(outer, low, high, top, bottom, weight):
    return pl.pallas_call(
        conv_kernel,
        out_shape=jax.ShapeDtypeStruct((2, 8, 1024), BF),
        in_specs=[whole()] * 6,
        out_specs=whole(),
        compiler_params=params(),
        name="conv",
    )(outer, low, high, top, bottom, weight)


def body(
    source_features,
    reference_features,
    interp,
    source_tile,
    source_block,
    conv_weight,
    grad_regularized,
):
    tiles = lax.axis_size("tile")
    views = lax.axis_size("view")
    view = lax.axis_index("view")
    up = [(i, i + 1) for i in range(tiles - 1)]
    down = [(i + 1, i) for i in range(tiles - 1)]

    def other(array, mask):
        return lax.ppermute(array, "view", [(i, i ^ mask) for i in range(views)])

    slots = jnp.arange(8, dtype=jnp.int32)
    y_low, core = view // 2, view % 2
    order = (
        ((slots // 2) % 2 ^ 1 ^ y_low) * 4 + ((slots // 4) ^ 1 ^ core) * 2 + slots % 2
    ).astype(jnp.int32)
    place = ((source_tile + 1) * 16 + source_block).reshape(-1)

    where = jnp.stack([y_low, core]).astype(jnp.int32)
    own = grad_regularized
    parts = (own, other(own, 1), other(own, 2), other(own, 3))
    operand = strips(source_features.reshape(1280, 128))
    cotangent, last, initial = slots_of(parts)
    operand, last, initial = lax.optimization_barrier((operand, last, initial))
    arrived = lax.all_to_all(operand, "tile", split_axis=0, concat_axis=0, tiled=True)
    top = lax.ppermute(last, "tile", up)
    bottom = lax.ppermute(initial, "tile", down)
    back_weight = conv_weight.transpose(1, 4, 0, 2, 3).reshape(96, 72)
    weight = conv_weight.transpose(0, 1, 3, 2, 4).reshape(72, 96)
    grad = grad_cost(view.astype(jnp.int32).reshape(1), cotangent, top, bottom, back_weight)
    arrived, grad, weight = lax.optimization_barrier((arrived, grad, weight))

    blocks, first_o, second_o, warped_o = warp_other(place, order, arrived, interp)
    first_m, second_m, warped_m = warp_mine(place, order, blocks, interp)
    first_chip, first_send = chip_first(first_m, other(first_o, 1))
    first_there = other(first_send, 2)
    second_own, second_send = chip_second(where, second_m, other(second_o, 1))
    second_there = other(second_send, 2)
    first_there, second_own = lax.optimization_barrier((first_there, second_own))
    mean_mine = mean_of(first_chip, first_there, reference_features)
    mean_other = other(mean_mine, 1)

    shared = (place, order, warped_o, warped_m, interp, mean_other, mean_mine, grad)
    landed = land_first((0, 1, 2, 3), *shared)
    landed, second_there = lax.optimization_barrier((landed, second_there))
    low, high, send = cost_of(
        where, first_chip, first_there, second_own, second_there, reference_features
    )
    near = other(send, 1)
    landed = land_last((4,), *shared, landed)
    landed, near = lax.optimization_barrier((landed, near))
    outer, cost_last, cost_initial = edges_of(where, low, high, near)
    landed, cost_last, cost_initial = lax.optimization_barrier((landed, cost_last, cost_initial))
    returned = lax.all_to_all(landed, "tile", split_axis=0, concat_axis=0, tiled=True)
    cost_top = lax.ppermute(cost_last, "tile", up)
    cost_bottom = lax.ppermute(cost_initial, "tile", down)
    regularized = conv(outer, low, high, cost_top, cost_bottom, weight)

    grad_source = unstrips(returned).reshape(source_features.shape)
    return regularized, grad_source


def solution(mesh):
    return jax.shard_map(
        body,
        mesh=mesh,
        in_specs=(
            P("view", None, "tile", None),
            P(None, "tile"),
            P("view", None, None, None, None),
            P("view", None, "tile", None),
            P("view", None, "tile", None),
            P(),
            P("view", None, "tile"),
        ),
        out_specs=(P("view", None, "tile"), P("view", None, "tile", None)),
        check_vma=False,
    )
```

```python
import functools

import jax
import jax.numpy as jnp
from jax import lax
from jax.experimental import pallas as pl
from jax.experimental.pallas import tpu as pltpu
from jax.sharding import PartitionSpec as P

BF = jnp.bfloat16
F32 = jnp.float32
VIEWS = 5
PLANES = 8
COUNT = 21.0
SEGS = 48
VMEM_LIMIT = 4 * 1024 * 1024
NT = (((1,), (1,)), ((), ()))
NN = (((1,), (0,)), ((), ()))
TN = (((0,), (0,)), ((), ()))


def params():
    return pltpu.CompilerParams(vmem_limit_bytes=VMEM_LIMIT)


def whole():
    return pl.BlockSpec(memory_space=pltpu.VMEM)


SMALL = pl.CostEstimate(flops=1000, bytes_accessed=1000, transcendentals=0)


def iota(shape, dim):
    return lax.broadcasted_iota(jnp.int32, shape, dim)


def band_table():
    row, lane = iota((96, 128), 0), iota((96, 128), 1)
    return ((lane >> 2) == (row & 31) + (row >> 5) - 1).astype(F32).astype(BF)


def row_mask():
    return (iota((128, 128), 0) >> 5) == (iota((128, 128), 1) & 3)


def strips_kernel(src_hbm, out_hbm, source, wide, stage, moved_out, in_sem, out_sem):
    loads = []
    for v in range(VIEWS):
        rows = pl.ds(v * 256, 256)
        loads.append(pltpu.make_async_copy(src_hbm.at[rows], source.at[rows], in_sem.at[v]))
        loads[-1].start()
    table = band_table()
    mask = row_mask()
    stores = []
    for v in range(VIEWS):
        loads[v].wait()
        wide[v] = source[v * 256 : (v + 1) * 256].astype(F32)
        for x in range(8):
            own = wide[v, pl.ds(x, 32, stride=8), :]
            tall = jnp.where(mask, jnp.concatenate([own] * 4, axis=0), 0.0).astype(BF)
            moved = lax.dot_general(table, tall, NT, preferred_element_type=F32)
            for band in range(3):
                stage[v * 3 + band, pl.ds(x, 32, stride=8), :] = moved[
                    band * 32 : (band + 1) * 32
                ]
        for band in range(3):
            moved_out[v, :, band * 128 : (band + 1) * 128] = stage[v * 3 + band].astype(BF)
        stores.append(
            pltpu.make_async_copy(
                moved_out.at[v], out_hbm.at[:, v * 384 : (v + 1) * 384], out_sem.at[v]
            )
        )
        stores[-1].start()
    for store in stores:
        store.wait()


def strips(source):
    return pl.pallas_call(
        strips_kernel,
        out_shape=pltpu.HBM((256, VIEWS * 384), BF),
        in_specs=[pl.BlockSpec(memory_space=pltpu.HBM)],
        out_specs=pl.BlockSpec(memory_space=pltpu.HBM),
        scratch_shapes=[
            pltpu.VMEM((1280, 128), BF),
            pltpu.VMEM((VIEWS, 256, 128), F32),
            pltpu.VMEM((VIEWS * 3, 256, 128), F32),
            pltpu.VMEM((VIEWS, 256, 384), BF),
            pltpu.SemaphoreType.DMA((VIEWS,)),
            pltpu.SemaphoreType.DMA((VIEWS,)),
        ],
        compiler_params=pltpu.CompilerParams(vmem_limit_bytes=2 * VMEM_LIMIT),
        name="strips",
    )(pltpu.with_memory_space_constraint(source, pltpu.HBM))


def unstrips_kernel(in_ref, out_ref, wide):
    for piece in range(VIEWS * 3):
        wide[piece] = in_ref[:, piece * 128 : (piece + 1) * 128].astype(F32)
    table = band_table()
    mask = row_mask()
    for x in range(8):
        columns = []
        for v in range(VIEWS):
            bands = [wide[v * 3 + band, pl.ds(x, 32, stride=8), :] for band in range(3)]
            columns.append(jnp.concatenate(bands, axis=0).astype(BF))
        stacked = jnp.concatenate(columns, axis=1)
        moved = lax.dot_general(stacked, table, TN, preferred_element_type=F32)
        parts = []
        for v in range(VIEWS):
            part = jnp.where(mask, moved[v * 128 : (v + 1) * 128], 0.0)
            parts.append((part[0:32] + part[32:64]) + (part[64:96] + part[96:128]))
        out_ref[pl.ds(x, 160, stride=8), :] = jnp.concatenate(parts, axis=0)


def unstrips(arrived):
    return pl.pallas_call(
        unstrips_kernel,
        out_shape=jax.ShapeDtypeStruct((1280, 128), F32),
        in_specs=[whole()],
        out_specs=whole(),
        scratch_shapes=[pltpu.VMEM((VIEWS * 3, 256, 128), F32)],
        compiler_params=params(),
        name="unstrips",
    )(arrived)


def half_mask(rows):
    return iota((rows, 128), 1) < 64


def spread_interp(values):
    parts = []
    zero = jnp.zeros((64, 64), BF)
    for k in range(4):
        parts.append(jnp.concatenate([values[k], zero], axis=1))
        parts.append(jnp.concatenate([zero, values[k]], axis=1))
    return jnp.concatenate(parts, axis=0)


def pair_swap(low, high):
    mask = half_mask(low.shape[0])
    first = jnp.where(mask, low, pltpu.roll(high, 64, 1))
    second = jnp.where(mask, pltpu.roll(low, 64, 1), high)
    return first, second


def turn_kernel(in_ref, blocks_ref):
    for view in range(VIEWS):
        turned = in_ref[:, view * 384 : (view + 1) * 384].astype(F32).T
        for band_row in range(12):
            upper = turned[band_row * 32 : band_row * 32 + 16]
            lower = turned[band_row * 32 + 16 : band_row * 32 + 32]
            for half in range(2):
                even, odd = pair_swap(
                    upper[:, half * 128 : half * 128 + 128], lower[:, half * 128 : half * 128 + 128]
                )
                at = view * SEGS + band_row * 4 + half * 2
                blocks_ref[at] = even.astype(BF)
                blocks_ref[at + 1] = odd.astype(BF)


def warp_planes(group, place_ref, order_ref, blocks_ref, interp_ref, first_ref, second_ref, warped_ref):
    first_ref[...] = jnp.zeros_like(first_ref)
    second_ref[...] = jnp.zeros_like(second_ref)

    def step(view, unused):
        for e in range(4):
            plane = order_ref[group * 4 + e]
            base = (view * PLANES + plane) * 64
            rows = []
            for g in range(16):
                taps = [blocks_ref[view * SEGS + place_ref[base + g * 4 + k]] for k in range(4)]
                rows.append(jnp.concatenate(taps, axis=1))
            picked = jnp.concatenate(rows, axis=0)
            matrix = spread_interp(interp_ref[view, plane])
            warped = lax.dot_general(picked, matrix, NN, preferred_element_type=F32)
            first_ref[e] += warped
            second_ref[e] += warped * warped
            warped_ref[view, e] = warped.astype(BF)
        return unused

    lax.fori_loop(0, VIEWS, step, 0, unroll=UNROLL)


def warp_other_kernel(
    place_ref, order_ref, in_ref, interp_ref, blocks_ref, first_ref, second_ref, warped_ref
):
    turn_kernel(in_ref, blocks_ref)
    warp_planes(0, place_ref, order_ref, blocks_ref, interp_ref, first_ref, second_ref, warped_ref)


def warp_mine_kernel(
    place_ref, order_ref, blocks_ref, interp_ref, first_ref, second_ref, warped_ref
):
    warp_planes(1, place_ref, order_ref, blocks_ref, interp_ref, first_ref, second_ref, warped_ref)


UNROLL = 5
SUMS = jax.ShapeDtypeStruct((4, 256, 128), F32)
WARPED = jax.ShapeDtypeStruct((VIEWS, 4, 256, 128), BF)
BLOCKS = jax.ShapeDtypeStruct((VIEWS * SEGS, 16, 128), BF)


def smem():
    return pl.BlockSpec(memory_space=pltpu.SMEM)


def warp_other(place, order, arrived, interp):
    return pl.pallas_call(
        warp_other_kernel,
        in_specs=[smem(), smem(), whole(), whole()],
        out_specs=[whole()] * 4,
        out_shape=[BLOCKS, SUMS, SUMS, WARPED],
        compiler_params=params(),
        name="warp_other",
    )(place, order, arrived, interp)


def warp_mine(place, order, blocks, interp):
    return pl.pallas_call(
        warp_mine_kernel,
        in_specs=[smem(), smem(), whole(), whole()],
        out_specs=[whole()] * 3,
        out_shape=[SUMS, SUMS, WARPED],
        compiler_params=params(),
        name="warp_mine",
    )(place, order, blocks, interp)


CHAINS = 4


def land_views(
    views, place_ref, order_ref, warped_o, warped_m, interp_ref, mean_o, mean_m, grad_ref, out_ref, accs
):
    groups = ((warped_o, mean_o), (warped_m, mean_m))
    for view in views:
        for acc in accs:
            acc[...] = jnp.zeros_like(acc)
        for e in range(8):
            warped_ref, mean_ref = groups[e // 4]
            plane = order_ref[e]
            base = (view * PLANES + plane) * 64
            warped = warped_ref[view, e % 4].astype(F32)
            grad = (grad_ref[plane] * (warped - mean_ref[e % 4].astype(F32))).astype(BF)
            matrix = spread_interp(interp_ref[view, plane])
            spread = lax.dot_general(grad, matrix, NT, preferred_element_type=F32)
            for g in range(16):
                for k in range(4):
                    where = place_ref[base + g * 4 + k]
                    accs[k][where] += spread[g * 16 : (g + 1) * 16, k * 128 : (k + 1) * 128]
        bands = []
        for band_row in range(12):
            columns_up, columns_low = [], []
            for half in range(2):
                at = band_row * 4 + half * 2
                even = (accs[0][at] + accs[1][at]) + (accs[2][at] + accs[3][at])
                odd = (accs[0][at + 1] + accs[1][at + 1]) + (accs[2][at + 1] + accs[3][at + 1])
                up, low = pair_swap(even, odd)
                columns_up.append(up)
                columns_low.append(low)
            bands.append(jnp.concatenate(columns_up, axis=1))
            bands.append(jnp.concatenate(columns_low, axis=1))
        lane = (view - views[0]) * 384
        out_ref[:, lane : lane + 384] = jnp.concatenate(bands, axis=0).T.astype(BF)


def land_first_kernel(views, *refs):
    land_views(views, *refs[:9], refs[9:])


def land_last_kernel(views, *refs):
    earlier_ref, out_hbm, own_ref, sem = refs[8], refs[9], refs[10], refs[11]
    lanes = earlier_ref.shape[1]
    first = pltpu.make_async_copy(earlier_ref, out_hbm.at[:, 0:lanes], sem.at[0])
    first.start()
    land_views(views, *refs[:8], own_ref, refs[12:])
    last = pltpu.make_async_copy(own_ref, out_hbm.at[:, lanes : VIEWS * 384], sem.at[1])
    last.start()
    first.wait()
    last.wait()


ACCUMULATORS = [pltpu.VMEM((SEGS, 16, 128), F32)] * CHAINS


def land_first(views, *operands):
    return pl.pallas_call(
        functools.partial(land_first_kernel, views),
        in_specs=[smem(), smem()] + [whole()] * 6,
        out_specs=whole(),
        out_shape=jax.ShapeDtypeStruct((256, len(views) * 384), BF),
        scratch_shapes=ACCUMULATORS,
        compiler_params=params(),
        cost_estimate=SMALL,
        name="land_first",
    )(*operands)


def land_last(views, *operands):
    return pl.pallas_call(
        functools.partial(land_last_kernel, views),
        in_specs=[smem(), smem()] + [whole()] * 7,
        out_specs=pl.BlockSpec(memory_space=pltpu.HBM),
        out_shape=pltpu.HBM((256, VIEWS * 384), BF),
        scratch_shapes=[
            pltpu.VMEM((256, len(views) * 384), BF),
            pltpu.SemaphoreType.DMA((2,)),
        ]
        + ACCUMULATORS,
        compiler_params=params(),
        cost_estimate=SMALL,
        name="land_last",
    )(*operands)


def chip_first_kernel(mine_ref, arrived_ref, sum_ref, send_ref):
    total = mine_ref[...] + arrived_ref[...]
    sum_ref[...] = total
    send_ref[...] = total.astype(BF)


def chip_second_kernel(where_ref, mine_ref, arrived_ref, own_ref, send_ref):
    core = where_ref[1]
    own_ref[0:2] = mine_ref[2:4] + arrived_ref[2:4]
    own_ref[2] = mine_ref[core] + arrived_ref[core]
    send_ref[0:2] = mine_ref[0:2] + arrived_ref[0:2]
    send_ref[2] = mine_ref[2 + core] + arrived_ref[2 + core]


def chip_first(mine, arrived):
    return pl.pallas_call(
        chip_first_kernel,
        in_specs=[whole()] * 2,
        out_specs=[whole()] * 2,
        out_shape=[SUMS, jax.ShapeDtypeStruct(SUMS.shape, BF)],
        compiler_params=params(),
        name="chip_first",
    )(mine, arrived)


def chip_second(where, mine, arrived):
    return pl.pallas_call(
        chip_second_kernel,
        in_specs=[smem()] + [whole()] * 2,
        out_specs=[whole()] * 2,
        out_shape=[jax.ShapeDtypeStruct((3, 256, 128), F32)] * 2,
        compiler_params=params(),
        name="chip_second",
    )(where, mine, arrived)


def turned_reference(ref_ref, pair):
    lanes = slice(pair * 128, pair * 128 + 128)
    even, odd = pair_swap(ref_ref[0:16, lanes].astype(F32), ref_ref[16:32, lanes].astype(F32))
    return jnp.concatenate([even, odd], axis=0)


def mean_kernel(sum_ref, there_ref, ref_ref, mean_ref):
    for pair in range(8):
        rows = slice(pair * 32, pair * 32 + 32)
        ref = turned_reference(ref_ref, pair)
        for e in range(4):
            total = sum_ref[e, rows] + there_ref[e ^ 2, rows].astype(F32) + ref
            mean_ref[e, rows] = (total * (1.0 / COUNT)).astype(BF)


def mean_of(sums, there, reference):
    return pl.pallas_call(
        mean_kernel,
        in_specs=[whole()] * 3,
        out_specs=whole(),
        out_shape=jax.ShapeDtypeStruct(SUMS.shape, BF),
        compiler_params=params(),
        name="mean",
    )(sums, there, reference)


def cost_kernel(
    where_ref, first_ref, first_there, second_ref, second_there, ref_ref, low_ref, high_ref, send_ref
):
    y_low, core = where_ref[0], where_ref[1]
    inside = jnp.where(y_low == core, 1.0, 0.0)
    for pair in range(8):
        rows = slice(pair * 32, pair * 32 + 32)
        ref = turned_reference(ref_ref, pair)
        square = ref * ref

        def plane_cost(mine, there, slot):
            first = first_ref[mine, rows] + first_there[there, rows].astype(F32) + ref
            second = second_ref[slot, rows] + second_there[slot, rows] + square
            mean = first * (1.0 / COUNT)
            return second * (1.0 / COUNT) - mean * mean

        low = plane_cost(2, 0, 0)
        high = plane_cost(3, 1, 1)
        far = plane_cost(core, 2 + core, 2)
        low_ref[0, rows] = low.astype(BF)
        high_ref[0, rows] = high.astype(BF)
        send_ref[0, rows] = jnp.where(core == 1, low, high).astype(BF)
        send_ref[1, rows] = (far * inside).astype(BF)


def edges_kernel(where_ref, low_ref, high_ref, near_ref, outer_ref, last_ref, initial_ref):
    core = where_ref[1]
    outer_ref[0] = near_ref[1 - core]
    outer_ref[1] = near_ref[core]
    for local, plane in ((0, outer_ref[0]), (1, low_ref[0]), (2, high_ref[0]), (3, outer_ref[1])):
        last_ref[local] = plane[192:256]
        initial_ref[local] = plane[0:64]


PLANE = jax.ShapeDtypeStruct((1, 256, 128), BF)
PAIR = jax.ShapeDtypeStruct((2, 256, 128), BF)
EDGES = jax.ShapeDtypeStruct((4, 64, 128), BF)


def cost_of(where, first, first_there, second, second_there, reference):
    return pl.pallas_call(
        cost_kernel,
        in_specs=[smem()] + [whole()] * 5,
        out_specs=[whole()] * 3,
        out_shape=[PLANE, PLANE, PAIR],
        compiler_params=params(),
        name="cost",
    )(where, first, first_there, second, second_there, reference)


def edges_of(where, low, high, near):
    return pl.pallas_call(
        edges_kernel,
        in_specs=[smem()] + [whole()] * 3,
        out_specs=[whole()] * 3,
        out_shape=[PAIR, EDGES, EDGES],
        compiler_params=params(),
        name="edges",
    )(where, low, high, near)


def slots_kernel(*refs):
    for slot in range(4):
        refs[4][slot] = refs[slot][...]
        refs[5][slot] = refs[slot][:, :, 768:1024]
        refs[6][slot] = refs[slot][:, :, 0:256]


def slots_of(parts):
    row = jax.ShapeDtypeStruct((4, 2, 8, 256), BF)
    return pl.pallas_call(
        slots_kernel,
        in_specs=[whole()] * 4,
        out_specs=[whole()] * 3,
        out_shape=[jax.ShapeDtypeStruct((4, 2, 8, 1024), BF), row, row],
        compiler_params=params(),
        name="slots",
    )(*parts)


def shifted(values, offset):
    lanes = values.shape[1]
    col = iota(values.shape, 1) & 255
    if offset > 0:
        return jnp.where(col == 255, 0.0, pltpu.roll(values, lanes - 1, 1))
    return jnp.where(col == 0, 0.0, pltpu.roll(values, 1, 1))


def grad_cost_kernel(
    view_ref, own_ref, top_ref, bottom_ref, weight_ref, out_hbm, out_ref, sem
):
    view = view_ref[0]
    padded = []
    for plane in range(PLANES):
        slot = jnp.bitwise_xor(view, plane // 2)
        line = jnp.concatenate(
            [
                top_ref[slot, plane % 2].astype(F32),
                own_ref[slot, plane % 2].astype(F32),
                bottom_ref[slot, plane % 2].astype(F32),
            ],
            axis=1,
        )
        padded.append(jnp.concatenate([shifted(line, 1), line, shifted(line, -1)], axis=0))
    zero = jnp.zeros_like(padded[0])
    weight = weight_ref[...]
    stores = []
    for plane in range(PLANES):
        near = [padded[p] if 0 <= p < PLANES else zero for p in (plane + 1, plane, plane - 1)]
        result = lax.dot_general(
            weight, jnp.concatenate(near, axis=0).astype(BF), NN, preferred_element_type=F32
        )
        grad = result[0:32, 512:1536] + result[32:64, 256:1280] + result[64:96, 0:1024]
        grad = grad * (2.0 / COUNT)
        for pair in range(8):
            upper = grad[0:16, pair * 128 : pair * 128 + 128]
            lower = grad[16:32, pair * 128 : pair * 128 + 128]
            even, odd = pair_swap(upper, lower)
            out_ref[plane, pair * 32 : pair * 32 + 16] = even
            out_ref[plane, pair * 32 + 16 : pair * 32 + 32] = odd
        if plane % 4 == 3:
            part = pl.ds(plane - 3, 4)
            stores.append(
                pltpu.make_async_copy(out_ref.at[part], out_hbm.at[part], sem.at[plane // 4])
            )
            stores[-1].start()
    for store in stores:
        store.wait()


def grad_cost(view, own, top, bottom, weight):
    return pl.pallas_call(
        grad_cost_kernel,
        out_shape=pltpu.HBM((PLANES, 256, 128), F32),
        in_specs=[pl.BlockSpec(memory_space=pltpu.SMEM)] + [whole()] * 4,
        out_specs=pl.BlockSpec(memory_space=pltpu.HBM),
        scratch_shapes=[pltpu.VMEM((PLANES, 256, 128), F32), pltpu.SemaphoreType.DMA((2,))],
        compiler_params=params(),
        name="grad_cost",
    )(view, own, top, bottom, weight)


def line_of(tall, pairs):
    upper, lower = [], []
    for pair in range(pairs):
        up, low = pair_swap(
            tall[pair * 32 : pair * 32 + 16], tall[pair * 32 + 16 : pair * 32 + 32]
        )
        upper.append(up)
        lower.append(low)
    return jnp.concatenate(
        [jnp.concatenate(upper, axis=1), jnp.concatenate(lower, axis=1)], axis=0
    )


def convolved(weight, line):
    wide = jnp.concatenate([shifted(line, -1), line, shifted(line, 1)], axis=0).astype(BF)
    return lax.dot_general(weight, wide, NN, preferred_element_type=F32)


def conv_kernel(outer_ref, low_ref, high_ref, weight_ref, out_ref):
    weight = weight_ref[...]
    results = []
    for plane in (outer_ref[0], low_ref[0], high_ref[0], outer_ref[1]):
        results.append(convolved(weight, line_of(plane.astype(F32), 8)))
    zero = jnp.zeros((8, 256), F32)
    for plane in range(2):
        total = None
        for a in range(3):
            same = results[plane + a][a * 24 + 8 : a * 24 + 16]
            above = results[plane + a][a * 24 : a * 24 + 8, 0:768]
            below = results[plane + a][a * 24 + 16 : a * 24 + 24, 256:1024]
            part = (
                same
                + jnp.concatenate([zero, above], axis=1)
                + jnp.concatenate([below, zero], axis=1)
            )
            total = part if total is None else total + part
        out_ref[plane] = total


def conv_rows_kernel(main_ref, top_ref, bottom_ref, weight_ref, out_ref):
    weight = weight_ref[...]
    results = []
    for local in range(4):
        tall = jnp.concatenate([top_ref[local], bottom_ref[local]], axis=0).astype(F32)
        results.append(convolved(weight, line_of(tall, 4)))
    for plane in range(2):
        first = main_ref[plane, :, 0:256]
        last = main_ref[plane, :, 768:1024]
        for a in range(3):
            first = first + results[plane + a][a * 24 : a * 24 + 8, 0:256]
            last = last + results[plane + a][a * 24 + 16 : a * 24 + 24, 256:512]
        out_ref[plane] = jnp.concatenate(
            [first, main_ref[plane, :, 256:768], last], axis=1
        ).astype(BF)


def conv(outer, low, high, weight):
    return pl.pallas_call(
        conv_kernel,
        out_shape=jax.ShapeDtypeStruct((2, 8, 1024), F32),
        in_specs=[whole()] * 4,
        out_specs=whole(),
        compiler_params=params(),
        name="conv",
    )(outer, low, high, weight)


def conv_rows(main, top, bottom, weight):
    return pl.pallas_call(
        conv_rows_kernel,
        out_shape=jax.ShapeDtypeStruct((2, 8, 1024), BF),
        in_specs=[whole()] * 4,
        out_specs=whole(),
        compiler_params=params(),
        name="conv_rows",
    )(main, top, bottom, weight)


def body(
    source_features,
    reference_features,
    interp,
    source_tile,
    source_block,
    conv_weight,
    grad_regularized,
):
    tiles = lax.axis_size("tile")
    views = lax.axis_size("view")
    view = lax.axis_index("view")
    up = [(i, i + 1) for i in range(tiles - 1)]
    down = [(i + 1, i) for i in range(tiles - 1)]

    def other(array, mask):
        return lax.ppermute(array, "view", [(i, i ^ mask) for i in range(views)])

    slots = jnp.arange(8, dtype=jnp.int32)
    y_low, core = view // 2, view % 2
    order = (
        ((slots // 2) % 2 ^ 1 ^ y_low) * 4 + ((slots // 4) ^ 1 ^ core) * 2 + slots % 2
    ).astype(jnp.int32)
    place = ((source_tile + 1) * 16 + source_block).reshape(-1)

    where = jnp.stack([y_low, core]).astype(jnp.int32)
    own = grad_regularized
    parts = (own, other(own, 1), other(own, 2), other(own, 3))
    operand = strips(source_features.reshape(1280, 128))
    cotangent, last, initial = slots_of(parts)
    operand, last, initial = lax.optimization_barrier((operand, last, initial))
    arrived = lax.all_to_all(operand, "tile", split_axis=0, concat_axis=0, tiled=True)
    top = lax.ppermute(last, "tile", up)
    bottom = lax.ppermute(initial, "tile", down)
    back_weight = conv_weight.transpose(1, 4, 0, 2, 3).reshape(96, 72)
    weight = conv_weight.transpose(0, 1, 3, 2, 4).reshape(72, 96)
    grad = grad_cost(view.astype(jnp.int32).reshape(1), cotangent, top, bottom, back_weight)
    arrived, grad, weight = lax.optimization_barrier((arrived, grad, weight))

    blocks, first_o, second_o, warped_o = warp_other(place, order, arrived, interp)
    first_m, second_m, warped_m = warp_mine(place, order, blocks, interp)
    first_chip, first_send = chip_first(first_m, other(first_o, 1))
    first_there = other(first_send, 2)
    second_own, second_send = chip_second(where, second_m, other(second_o, 1))
    second_there = other(second_send, 2)
    first_there, second_own = lax.optimization_barrier((first_there, second_own))
    mean_mine = mean_of(first_chip, first_there, reference_features)
    mean_other = other(mean_mine, 1)

    shared = (place, order, warped_o, warped_m, interp, mean_other, mean_mine, grad)
    landed = land_first((0, 1, 2, 3), *shared)
    landed, second_there = lax.optimization_barrier((landed, second_there))
    low, high, send = cost_of(
        where, first_chip, first_there, second_own, second_there, reference_features
    )
    near = other(send, 1)
    landed = land_last((4,), *shared, landed)
    landed, near = lax.optimization_barrier((landed, near))
    outer, cost_last, cost_initial = edges_of(where, low, high, near)
    landed, cost_last, cost_initial = lax.optimization_barrier((landed, cost_last, cost_initial))
    returned = lax.all_to_all(landed, "tile", split_axis=0, concat_axis=0, tiled=True)
    cost_top = lax.ppermute(cost_last, "tile", up)
    cost_bottom = lax.ppermute(cost_initial, "tile", down)
    regularized = conv_rows(conv(outer, low, high, weight), cost_top, cost_bottom, weight)

    grad_source = unstrips(returned).reshape(source_features.shape)
    return regularized, grad_source


def solution(mesh):
    return jax.shard_map(
        body,
        mesh=mesh,
        in_specs=(
            P("view", None, "tile", None),
            P(None, "tile"),
            P("view", None, None, None, None),
            P("view", None, "tile", None),
            P("view", None, "tile", None),
            P(),
            P("view", None, "tile"),
        ),
        out_specs=(P("view", None, "tile"), P("view", None, "tile", None)),
        check_vma=False,
    )
```

```python
import functools

import jax
import jax.numpy as jnp
from jax import lax
from jax.experimental import pallas as pl
from jax.experimental.pallas import tpu as pltpu
from jax.sharding import PartitionSpec as P

BF = jnp.bfloat16
F32 = jnp.float32
VIEWS = 5
PLANES = 8
COUNT = 21.0
SEGS = 48
VMEM_LIMIT = 4 * 1024 * 1024
NT = (((1,), (1,)), ((), ()))
NN = (((1,), (0,)), ((), ()))
TN = (((0,), (0,)), ((), ()))


def params():
    return pltpu.CompilerParams(vmem_limit_bytes=VMEM_LIMIT)


def whole():
    return pl.BlockSpec(memory_space=pltpu.VMEM)


SMALL = pl.CostEstimate(flops=1000, bytes_accessed=1000, transcendentals=0)


def iota(shape, dim):
    return lax.broadcasted_iota(jnp.int32, shape, dim)


def band_table():
    row, lane = iota((96, 128), 0), iota((96, 128), 1)
    return ((lane >> 2) == (row & 31) + (row >> 5) - 1).astype(F32).astype(BF)


def row_mask():
    return (iota((128, 128), 0) >> 5) == (iota((128, 128), 1) & 3)


def strips_kernel(src_ref, out_ref, wide, stage):
    wide[...] = src_ref[...].astype(F32)
    table = band_table()
    mask = row_mask()
    for x in range(8):
        own = wide[pl.ds(x, 160, stride=8), :]
        parts = []
        for v in range(VIEWS):
            part = own[v * 32 : (v + 1) * 32]
            parts.append(jnp.where(mask, jnp.concatenate([part] * 4, axis=0), 0.0).astype(BF))
        stacked = jnp.concatenate(parts, axis=0)
        moved = lax.dot_general(table, stacked, NT, preferred_element_type=F32)
        for v in range(VIEWS):
            for band in range(3):
                stage[v * 3 + band, pl.ds(x, 32, stride=8), :] = moved[
                    band * 32 : (band + 1) * 32, v * 128 : (v + 1) * 128
                ]
    for piece in range(VIEWS * 3):
        out_ref[:, piece * 128 : (piece + 1) * 128] = stage[piece].astype(BF)


def strips(source):
    return pl.pallas_call(
        strips_kernel,
        out_shape=jax.ShapeDtypeStruct((256, VIEWS * 384), BF),
        in_specs=[whole()],
        out_specs=whole(),
        scratch_shapes=[pltpu.VMEM((1280, 128), F32), pltpu.VMEM((VIEWS * 3, 256, 128), F32)],
        compiler_params=params(),
        name="strips",
    )(source)


def unstrips_kernel(in_ref, out_ref, wide):
    for piece in range(VIEWS * 3):
        wide[piece] = in_ref[:, piece * 128 : (piece + 1) * 128].astype(F32)
    table = band_table()
    mask = row_mask()
    for x in range(8):
        columns = []
        for v in range(VIEWS):
            bands = [wide[v * 3 + band, pl.ds(x, 32, stride=8), :] for band in range(3)]
            columns.append(jnp.concatenate(bands, axis=0).astype(BF))
        stacked = jnp.concatenate(columns, axis=1)
        moved = lax.dot_general(stacked, table, TN, preferred_element_type=F32)
        parts = []
        for v in range(VIEWS):
            part = jnp.where(mask, moved[v * 128 : (v + 1) * 128], 0.0)
            parts.append((part[0:32] + part[32:64]) + (part[64:96] + part[96:128]))
        out_ref[pl.ds(x, 160, stride=8), :] = jnp.concatenate(parts, axis=0)


def unstrips(arrived):
    return pl.pallas_call(
        unstrips_kernel,
        out_shape=jax.ShapeDtypeStruct((1280, 128), F32),
        in_specs=[whole()],
        out_specs=whole(),
        scratch_shapes=[pltpu.VMEM((VIEWS * 3, 256, 128), F32)],
        compiler_params=params(),
        name="unstrips",
    )(arrived)


def half_mask(rows):
    return iota((rows, 128), 1) < 64


def spread_interp(values):
    parts = []
    zero = jnp.zeros((64, 64), BF)
    for k in range(4):
        parts.append(jnp.concatenate([values[k], zero], axis=1))
        parts.append(jnp.concatenate([zero, values[k]], axis=1))
    return jnp.concatenate(parts, axis=0)


def pair_swap(low, high):
    mask = half_mask(low.shape[0])
    first = jnp.where(mask, low, pltpu.roll(high, 64, 1))
    second = jnp.where(mask, pltpu.roll(low, 64, 1), high)
    return first, second


def turn_kernel(in_ref, blocks_ref):
    for view in range(VIEWS):
        turned = in_ref[:, view * 384 : (view + 1) * 384].astype(F32).T
        for band_row in range(12):
            upper = turned[band_row * 32 : band_row * 32 + 16]
            lower = turned[band_row * 32 + 16 : band_row * 32 + 32]
            for half in range(2):
                even, odd = pair_swap(
                    upper[:, half * 128 : half * 128 + 128], lower[:, half * 128 : half * 128 + 128]
                )
                at = view * SEGS + band_row * 4 + half * 2
                blocks_ref[at] = even.astype(BF)
                blocks_ref[at + 1] = odd.astype(BF)


def warp_planes(group, place_ref, order_ref, blocks_ref, interp_ref, first_ref, second_ref, warped_ref):
    first_ref[...] = jnp.zeros_like(first_ref)
    second_ref[...] = jnp.zeros_like(second_ref)

    def step(view, unused):
        for e in range(4):
            plane = order_ref[group * 4 + e]
            base = (view * PLANES + plane) * 64
            rows = []
            for g in range(16):
                taps = [blocks_ref[view * SEGS + place_ref[base + g * 4 + k]] for k in range(4)]
                rows.append(jnp.concatenate(taps, axis=1))
            picked = jnp.concatenate(rows, axis=0)
            matrix = spread_interp(interp_ref[view, plane])
            warped = lax.dot_general(picked, matrix, NN, preferred_element_type=F32)
            first_ref[e] += warped
            second_ref[e] += warped * warped
            warped_ref[view, e] = warped.astype(BF)
        return unused

    lax.fori_loop(0, VIEWS, step, 0, unroll=UNROLL)


def warp_other_kernel(
    place_ref, order_ref, in_ref, interp_ref, blocks_ref, first_ref, second_ref, warped_ref
):
    turn_kernel(in_ref, blocks_ref)
    warp_planes(0, place_ref, order_ref, blocks_ref, interp_ref, first_ref, second_ref, warped_ref)


def warp_mine_kernel(
    place_ref, order_ref, blocks_ref, interp_ref, first_ref, second_ref, warped_ref
):
    warp_planes(1, place_ref, order_ref, blocks_ref, interp_ref, first_ref, second_ref, warped_ref)


UNROLL = 5
SUMS = jax.ShapeDtypeStruct((4, 256, 128), F32)
WARPED = jax.ShapeDtypeStruct((VIEWS, 4, 256, 128), BF)
BLOCKS = jax.ShapeDtypeStruct((VIEWS * SEGS, 16, 128), BF)


def smem():
    return pl.BlockSpec(memory_space=pltpu.SMEM)


def warp_other(place, order, arrived, interp):
    return pl.pallas_call(
        warp_other_kernel,
        in_specs=[smem(), smem(), whole(), whole()],
        out_specs=[whole()] * 4,
        out_shape=[BLOCKS, SUMS, SUMS, WARPED],
        compiler_params=params(),
        name="warp_other",
    )(place, order, arrived, interp)


def warp_mine(place, order, blocks, interp):
    return pl.pallas_call(
        warp_mine_kernel,
        in_specs=[smem(), smem(), whole(), whole()],
        out_specs=[whole()] * 3,
        out_shape=[SUMS, SUMS, WARPED],
        compiler_params=params(),
        name="warp_mine",
    )(place, order, blocks, interp)


CHAINS = 4


def land_views(
    views, place_ref, order_ref, warped_o, warped_m, interp_ref, mean_o, mean_m, grad_ref, out_ref, accs
):
    groups = ((warped_o, mean_o), (warped_m, mean_m))
    for view in views:
        for acc in accs:
            acc[...] = jnp.zeros_like(acc)
        for e in range(8):
            warped_ref, mean_ref = groups[e // 4]
            plane = order_ref[e]
            base = (view * PLANES + plane) * 64
            warped = warped_ref[view, e % 4].astype(F32)
            grad = (grad_ref[plane] * (warped - mean_ref[e % 4].astype(F32))).astype(BF)
            matrix = spread_interp(interp_ref[view, plane])
            spread = lax.dot_general(grad, matrix, NT, preferred_element_type=F32)
            for g in range(16):
                for k in range(4):
                    where = place_ref[base + g * 4 + k]
                    accs[k][where] += spread[g * 16 : (g + 1) * 16, k * 128 : (k + 1) * 128]
        bands = []
        for band_row in range(12):
            columns_up, columns_low = [], []
            for half in range(2):
                at = band_row * 4 + half * 2
                even = (accs[0][at] + accs[1][at]) + (accs[2][at] + accs[3][at])
                odd = (accs[0][at + 1] + accs[1][at + 1]) + (accs[2][at + 1] + accs[3][at + 1])
                up, low = pair_swap(even, odd)
                columns_up.append(up)
                columns_low.append(low)
            bands.append(jnp.concatenate(columns_up, axis=1))
            bands.append(jnp.concatenate(columns_low, axis=1))
        lane = (view - views[0]) * 384
        out_ref[:, lane : lane + 384] = jnp.concatenate(bands, axis=0).T.astype(BF)


def land_first_kernel(views, *refs):
    land_views(views, *refs[:9], refs[9:])


def land_last_kernel(views, *refs):
    earlier_ref, out_hbm, own_ref, sem = refs[8], refs[9], refs[10], refs[11]
    lanes = earlier_ref.shape[1]
    first = pltpu.make_async_copy(earlier_ref, out_hbm.at[:, 0:lanes], sem.at[0])
    first.start()
    land_views(views, *refs[:8], own_ref, refs[12:])
    last = pltpu.make_async_copy(own_ref, out_hbm.at[:, lanes : VIEWS * 384], sem.at[1])
    last.start()
    first.wait()
    last.wait()


ACCUMULATORS = [pltpu.VMEM((SEGS, 16, 128), F32)] * CHAINS


def land_first(views, *operands):
    return pl.pallas_call(
        functools.partial(land_first_kernel, views),
        in_specs=[smem(), smem()] + [whole()] * 6,
        out_specs=whole(),
        out_shape=jax.ShapeDtypeStruct((256, len(views) * 384), BF),
        scratch_shapes=ACCUMULATORS,
        compiler_params=params(),
        cost_estimate=SMALL,
        name="land_first",
    )(*operands)


def land_last(views, *operands):
    return pl.pallas_call(
        functools.partial(land_last_kernel, views),
        in_specs=[smem(), smem()] + [whole()] * 7,
        out_specs=pl.BlockSpec(memory_space=pltpu.HBM),
        out_shape=pltpu.HBM((256, VIEWS * 384), BF),
        scratch_shapes=[
            pltpu.VMEM((256, len(views) * 384), BF),
            pltpu.SemaphoreType.DMA((2,)),
        ]
        + ACCUMULATORS,
        compiler_params=params(),
        cost_estimate=SMALL,
        name="land_last",
    )(*operands)


def chip_first_kernel(mine_ref, arrived_ref, sum_ref, send_ref):
    total = mine_ref[...] + arrived_ref[...]
    sum_ref[...] = total
    send_ref[...] = total.astype(BF)


def chip_second_kernel(where_ref, mine_ref, arrived_ref, own_ref, send_ref):
    core = where_ref[1]
    own_ref[0:2] = mine_ref[2:4] + arrived_ref[2:4]
    own_ref[2] = mine_ref[core] + arrived_ref[core]
    send_ref[0:2] = mine_ref[0:2] + arrived_ref[0:2]
    send_ref[2] = mine_ref[2 + core] + arrived_ref[2 + core]


def chip_first(mine, arrived):
    return pl.pallas_call(
        chip_first_kernel,
        in_specs=[whole()] * 2,
        out_specs=[whole()] * 2,
        out_shape=[SUMS, jax.ShapeDtypeStruct(SUMS.shape, BF)],
        compiler_params=params(),
        name="chip_first",
    )(mine, arrived)


def chip_second(where, mine, arrived):
    return pl.pallas_call(
        chip_second_kernel,
        in_specs=[smem()] + [whole()] * 2,
        out_specs=[whole()] * 2,
        out_shape=[jax.ShapeDtypeStruct((3, 256, 128), F32)] * 2,
        compiler_params=params(),
        name="chip_second",
    )(where, mine, arrived)


def turned_reference(ref_ref, pair):
    lanes = slice(pair * 128, pair * 128 + 128)
    even, odd = pair_swap(ref_ref[0:16, lanes].astype(F32), ref_ref[16:32, lanes].astype(F32))
    return jnp.concatenate([even, odd], axis=0)


def mean_kernel(sum_ref, there_ref, ref_ref, mean_ref):
    for pair in range(8):
        rows = slice(pair * 32, pair * 32 + 32)
        ref = turned_reference(ref_ref, pair)
        for e in range(4):
            total = sum_ref[e, rows] + there_ref[e ^ 2, rows].astype(F32) + ref
            mean_ref[e, rows] = (total * (1.0 / COUNT)).astype(BF)


def mean_of(sums, there, reference):
    return pl.pallas_call(
        mean_kernel,
        in_specs=[whole()] * 3,
        out_specs=whole(),
        out_shape=jax.ShapeDtypeStruct(SUMS.shape, BF),
        compiler_params=params(),
        name="mean",
    )(sums, there, reference)


def cost_kernel(
    where_ref, first_ref, first_there, second_ref, second_there, ref_ref, low_ref, high_ref, send_ref
):
    y_low, core = where_ref[0], where_ref[1]
    inside = jnp.where(y_low == core, 1.0, 0.0)
    for pair in range(8):
        rows = slice(pair * 32, pair * 32 + 32)
        ref = turned_reference(ref_ref, pair)
        square = ref * ref

        def plane_cost(mine, there, slot):
            first = first_ref[mine, rows] + first_there[there, rows].astype(F32) + ref
            second = second_ref[slot, rows] + second_there[slot, rows] + square
            mean = first * (1.0 / COUNT)
            return second * (1.0 / COUNT) - mean * mean

        low = plane_cost(2, 0, 0)
        high = plane_cost(3, 1, 1)
        far = plane_cost(core, 2 + core, 2)
        low_ref[0, rows] = low.astype(BF)
        high_ref[0, rows] = high.astype(BF)
        send_ref[0, rows] = jnp.where(core == 1, low, high).astype(BF)
        send_ref[1, rows] = (far * inside).astype(BF)


def edges_kernel(where_ref, low_ref, high_ref, near_ref, outer_ref, last_ref, initial_ref):
    core = where_ref[1]
    outer_ref[0] = near_ref[1 - core]
    outer_ref[1] = near_ref[core]
    for local, plane in ((0, outer_ref[0]), (1, low_ref[0]), (2, high_ref[0]), (3, outer_ref[1])):
        last_ref[local] = plane[192:256]
        initial_ref[local] = plane[0:64]


PLANE = jax.ShapeDtypeStruct((1, 256, 128), BF)
PAIR = jax.ShapeDtypeStruct((2, 256, 128), BF)
EDGES = jax.ShapeDtypeStruct((4, 64, 128), BF)


def cost_of(where, first, first_there, second, second_there, reference):
    return pl.pallas_call(
        cost_kernel,
        in_specs=[smem()] + [whole()] * 5,
        out_specs=[whole()] * 3,
        out_shape=[PLANE, PLANE, PAIR],
        compiler_params=params(),
        name="cost",
    )(where, first, first_there, second, second_there, reference)


def edges_of(where, low, high, near):
    return pl.pallas_call(
        edges_kernel,
        in_specs=[smem()] + [whole()] * 3,
        out_specs=[whole()] * 3,
        out_shape=[PAIR, EDGES, EDGES],
        compiler_params=params(),
        name="edges",
    )(where, low, high, near)


def slots_kernel(*refs):
    for slot in range(4):
        refs[4][slot] = refs[slot][...]
        refs[5][slot] = refs[slot][:, :, 768:1024]
        refs[6][slot] = refs[slot][:, :, 0:256]


def slots_of(parts):
    row = jax.ShapeDtypeStruct((4, 2, 8, 256), BF)
    return pl.pallas_call(
        slots_kernel,
        in_specs=[whole()] * 4,
        out_specs=[whole()] * 3,
        out_shape=[jax.ShapeDtypeStruct((4, 2, 8, 1024), BF), row, row],
        compiler_params=params(),
        name="slots",
    )(*parts)


def shifted(values, offset):
    lanes = values.shape[1]
    col = iota(values.shape, 1) & 255
    if offset > 0:
        return jnp.where(col == 255, 0.0, pltpu.roll(values, lanes - 1, 1))
    return jnp.where(col == 0, 0.0, pltpu.roll(values, 1, 1))


def grad_cost_kernel(
    view_ref, own_ref, top_ref, bottom_ref, weight_ref, out_hbm, out_ref, sem
):
    view = view_ref[0]
    padded = []
    for plane in range(PLANES):
        slot = jnp.bitwise_xor(view, plane // 2)
        line = jnp.concatenate(
            [
                top_ref[slot, plane % 2].astype(F32),
                own_ref[slot, plane % 2].astype(F32),
                bottom_ref[slot, plane % 2].astype(F32),
            ],
            axis=1,
        )
        padded.append(jnp.concatenate([shifted(line, 1), line, shifted(line, -1)], axis=0))
    zero = jnp.zeros_like(padded[0])
    weight = weight_ref[...]
    stores = []
    for plane in range(PLANES):
        near = [padded[p] if 0 <= p < PLANES else zero for p in (plane + 1, plane, plane - 1)]
        result = lax.dot_general(
            weight, jnp.concatenate(near, axis=0).astype(BF), NN, preferred_element_type=F32
        )
        grad = result[0:32, 512:1536] + result[32:64, 256:1280] + result[64:96, 0:1024]
        grad = grad * (2.0 / COUNT)
        for pair in range(8):
            upper = grad[0:16, pair * 128 : pair * 128 + 128]
            lower = grad[16:32, pair * 128 : pair * 128 + 128]
            even, odd = pair_swap(upper, lower)
            out_ref[plane, pair * 32 : pair * 32 + 16] = even
            out_ref[plane, pair * 32 + 16 : pair * 32 + 32] = odd
        if plane % 2 == 1:
            part = pl.ds(plane - 1, 2)
            stores.append(
                pltpu.make_async_copy(out_ref.at[part], out_hbm.at[part], sem.at[plane // 2])
            )
            stores[-1].start()
    for store in stores:
        store.wait()


def grad_cost(view, own, top, bottom, weight):
    return pl.pallas_call(
        grad_cost_kernel,
        out_shape=pltpu.HBM((PLANES, 256, 128), F32),
        in_specs=[pl.BlockSpec(memory_space=pltpu.SMEM)] + [whole()] * 4,
        out_specs=pl.BlockSpec(memory_space=pltpu.HBM),
        scratch_shapes=[pltpu.VMEM((PLANES, 256, 128), F32), pltpu.SemaphoreType.DMA((4,))],
        compiler_params=params(),
        name="grad_cost",
    )(view, own, top, bottom, weight)


def line_of(tall, pairs):
    upper, lower = [], []
    for pair in range(pairs):
        up, low = pair_swap(
            tall[pair * 32 : pair * 32 + 16], tall[pair * 32 + 16 : pair * 32 + 32]
        )
        upper.append(up)
        lower.append(low)
    return jnp.concatenate(
        [jnp.concatenate(upper, axis=1), jnp.concatenate(lower, axis=1)], axis=0
    )


def convolved(weight, line):
    wide = jnp.concatenate([shifted(line, -1), line, shifted(line, 1)], axis=0).astype(BF)
    return lax.dot_general(weight, wide, NN, preferred_element_type=F32)


def conv_kernel(outer_ref, low_ref, high_ref, weight_ref, out_ref):
    weight = weight_ref[...]
    results = []
    for plane in (outer_ref[0], low_ref[0], high_ref[0], outer_ref[1]):
        results.append(convolved(weight, line_of(plane.astype(F32), 8)))
    zero = jnp.zeros((8, 256), F32)
    for plane in range(2):
        total = None
        for a in range(3):
            same = results[plane + a][a * 24 + 8 : a * 24 + 16]
            above = results[plane + a][a * 24 : a * 24 + 8, 0:768]
            below = results[plane + a][a * 24 + 16 : a * 24 + 24, 256:1024]
            part = (
                same
                + jnp.concatenate([zero, above], axis=1)
                + jnp.concatenate([below, zero], axis=1)
            )
            total = part if total is None else total + part
        out_ref[plane] = total


def conv_rows_kernel(main_ref, top_ref, bottom_ref, weight_ref, out_ref):
    weight = weight_ref[...]
    results = []
    for local in range(4):
        tall = jnp.concatenate([top_ref[local], bottom_ref[local]], axis=0).astype(F32)
        results.append(convolved(weight, line_of(tall, 4)))
    for plane in range(2):
        first = main_ref[plane, :, 0:256]
        last = main_ref[plane, :, 768:1024]
        for a in range(3):
            first = first + results[plane + a][a * 24 : a * 24 + 8, 0:256]
            last = last + results[plane + a][a * 24 + 16 : a * 24 + 24, 256:512]
        out_ref[plane] = jnp.concatenate(
            [first, main_ref[plane, :, 256:768], last], axis=1
        ).astype(BF)


def conv(outer, low, high, weight):
    return pl.pallas_call(
        conv_kernel,
        out_shape=jax.ShapeDtypeStruct((2, 8, 1024), F32),
        in_specs=[whole()] * 4,
        out_specs=whole(),
        compiler_params=params(),
        name="conv",
    )(outer, low, high, weight)


def conv_rows(main, top, bottom, weight):
    return pl.pallas_call(
        conv_rows_kernel,
        out_shape=jax.ShapeDtypeStruct((2, 8, 1024), BF),
        in_specs=[whole()] * 4,
        out_specs=whole(),
        compiler_params=params(),
        name="conv_rows",
    )(main, top, bottom, weight)


def body(
    source_features,
    reference_features,
    interp,
    source_tile,
    source_block,
    conv_weight,
    grad_regularized,
):
    tiles = lax.axis_size("tile")
    views = lax.axis_size("view")
    view = lax.axis_index("view")
    up = [(i, i + 1) for i in range(tiles - 1)]
    down = [(i + 1, i) for i in range(tiles - 1)]

    def other(array, mask):
        return lax.ppermute(array, "view", [(i, i ^ mask) for i in range(views)])

    slots = jnp.arange(8, dtype=jnp.int32)
    y_low, core = view // 2, view % 2
    order = (
        ((slots // 2) % 2 ^ 1 ^ y_low) * 4 + ((slots // 4) ^ 1 ^ core) * 2 + slots % 2
    ).astype(jnp.int32)
    place = ((source_tile + 1) * 16 + source_block).reshape(-1)

    where = jnp.stack([y_low, core]).astype(jnp.int32)
    own = grad_regularized
    parts = (own, other(own, 1), other(own, 2), other(own, 3))
    operand = strips(source_features.reshape(1280, 128))
    cotangent, last, initial = slots_of(parts)
    operand, last, initial = lax.optimization_barrier((operand, last, initial))
    arrived = lax.all_to_all(operand, "tile", split_axis=0, concat_axis=0, tiled=True)
    top = lax.ppermute(last, "tile", up)
    bottom = lax.ppermute(initial, "tile", down)
    back_weight = conv_weight.transpose(1, 4, 0, 2, 3).reshape(96, 72)
    weight = conv_weight.transpose(0, 1, 3, 2, 4).reshape(72, 96)
    grad = grad_cost(view.astype(jnp.int32).reshape(1), cotangent, top, bottom, back_weight)
    arrived, grad, weight = lax.optimization_barrier((arrived, grad, weight))

    blocks, first_o, second_o, warped_o = warp_other(place, order, arrived, interp)
    first_m, second_m, warped_m = warp_mine(place, order, blocks, interp)
    first_chip, first_send = chip_first(first_m, other(first_o, 1))
    first_there = other(first_send, 2)
    second_own, second_send = chip_second(where, second_m, other(second_o, 1))
    second_there = other(second_send, 2)
    first_there, second_own = lax.optimization_barrier((first_there, second_own))
    mean_mine = mean_of(first_chip, first_there, reference_features)
    mean_other = other(mean_mine, 1)

    shared = (place, order, warped_o, warped_m, interp, mean_other, mean_mine, grad)
    landed = land_first((0, 1, 2, 3), *shared)
    landed, second_there = lax.optimization_barrier((landed, second_there))
    low, high, send = cost_of(
        where, first_chip, first_there, second_own, second_there, reference_features
    )
    near = other(send, 1)
    landed = land_last((4,), *shared, landed)
    landed, near = lax.optimization_barrier((landed, near))
    outer, cost_last, cost_initial = edges_of(where, low, high, near)
    landed, cost_last, cost_initial = lax.optimization_barrier((landed, cost_last, cost_initial))
    returned = lax.all_to_all(landed, "tile", split_axis=0, concat_axis=0, tiled=True)
    cost_top = lax.ppermute(cost_last, "tile", up)
    cost_bottom = lax.ppermute(cost_initial, "tile", down)
    regularized = conv_rows(conv(outer, low, high, weight), cost_top, cost_bottom, weight)

    grad_source = unstrips(returned).reshape(source_features.shape)
    return regularized, grad_source


def solution(mesh):
    return jax.shard_map(
        body,
        mesh=mesh,
        in_specs=(
            P("view", None, "tile", None),
            P(None, "tile"),
            P("view", None, None, None, None),
            P("view", None, "tile", None),
            P("view", None, "tile", None),
            P(),
            P("view", None, "tile"),
        ),
        out_specs=(P("view", None, "tile"), P("view", None, "tile", None)),
        check_vma=False,
    )
```

```python
import functools

import jax
import jax.numpy as jnp
from jax import lax
from jax.experimental import pallas as pl
from jax.experimental.pallas import tpu as pltpu
from jax.sharding import PartitionSpec as P

BF = jnp.bfloat16
F32 = jnp.float32
VIEWS = 5
PLANES = 8
COUNT = 21.0
SEGS = 48
VMEM_LIMIT = 4 * 1024 * 1024
NT = (((1,), (1,)), ((), ()))
NN = (((1,), (0,)), ((), ()))
TN = (((0,), (0,)), ((), ()))


def params():
    return pltpu.CompilerParams(vmem_limit_bytes=VMEM_LIMIT)


def whole():
    return pl.BlockSpec(memory_space=pltpu.VMEM)


SMALL = pl.CostEstimate(flops=1000, bytes_accessed=1000, transcendentals=0)


def iota(shape, dim):
    return lax.broadcasted_iota(jnp.int32, shape, dim)


def band_table():
    row, lane = iota((96, 128), 0), iota((96, 128), 1)
    return ((lane >> 2) == (row & 31) + (row >> 5) - 1).astype(F32).astype(BF)


def row_mask():
    return (iota((128, 128), 0) >> 5) == (iota((128, 128), 1) & 3)


def strips_kernel(src_ref, out_ref, wide, stage):
    wide[...] = src_ref[...].astype(F32)
    table = band_table()
    mask = row_mask()
    for x in range(8):
        own = wide[pl.ds(x, 160, stride=8), :]
        parts = []
        for v in range(VIEWS):
            part = own[v * 32 : (v + 1) * 32]
            parts.append(jnp.where(mask, jnp.concatenate([part] * 4, axis=0), 0.0).astype(BF))
        stacked = jnp.concatenate(parts, axis=0)
        moved = lax.dot_general(table, stacked, NT, preferred_element_type=F32)
        for v in range(VIEWS):
            for band in range(3):
                stage[v * 3 + band, pl.ds(x, 32, stride=8), :] = moved[
                    band * 32 : (band + 1) * 32, v * 128 : (v + 1) * 128
                ]
    for piece in range(VIEWS * 3):
        out_ref[:, piece * 128 : (piece + 1) * 128] = stage[piece].astype(BF)


def strips(source):
    return pl.pallas_call(
        strips_kernel,
        out_shape=jax.ShapeDtypeStruct((256, VIEWS * 384), BF),
        in_specs=[whole()],
        out_specs=whole(),
        scratch_shapes=[pltpu.VMEM((1280, 128), F32), pltpu.VMEM((VIEWS * 3, 256, 128), F32)],
        compiler_params=params(),
        name="strips",
    )(source)


def unstrips_kernel(in_ref, out_ref, wide):
    for piece in range(VIEWS * 3):
        wide[piece] = in_ref[:, piece * 128 : (piece + 1) * 128].astype(F32)
    table = band_table()
    mask = row_mask()
    for x in range(8):
        columns = []
        for v in range(VIEWS):
            bands = [wide[v * 3 + band, pl.ds(x, 32, stride=8), :] for band in range(3)]
            columns.append(jnp.concatenate(bands, axis=0).astype(BF))
        stacked = jnp.concatenate(columns, axis=1)
        moved = lax.dot_general(stacked, table, TN, preferred_element_type=F32)
        parts = []
        for v in range(VIEWS):
            part = jnp.where(mask, moved[v * 128 : (v + 1) * 128], 0.0)
            parts.append((part[0:32] + part[32:64]) + (part[64:96] + part[96:128]))
        out_ref[pl.ds(x, 160, stride=8), :] = jnp.concatenate(parts, axis=0)


def unstrips(arrived):
    return pl.pallas_call(
        unstrips_kernel,
        out_shape=jax.ShapeDtypeStruct((1280, 128), F32),
        in_specs=[whole()],
        out_specs=whole(),
        scratch_shapes=[pltpu.VMEM((VIEWS * 3, 256, 128), F32)],
        compiler_params=params(),
        name="unstrips",
    )(arrived)


def half_mask(rows):
    return iota((rows, 128), 1) < 64


def spread_interp(values):
    parts = []
    zero = jnp.zeros((64, 64), BF)
    for k in range(4):
        parts.append(jnp.concatenate([values[k], zero], axis=1))
        parts.append(jnp.concatenate([zero, values[k]], axis=1))
    return jnp.concatenate(parts, axis=0)


def pair_swap(low, high):
    mask = half_mask(low.shape[0])
    first = jnp.where(mask, low, pltpu.roll(high, 64, 1))
    second = jnp.where(mask, pltpu.roll(low, 64, 1), high)
    return first, second


def turn_kernel(in_ref, blocks_ref):
    for view in range(VIEWS):
        turned = in_ref[:, view * 384 : (view + 1) * 384].astype(F32).T
        for band_row in range(12):
            upper = turned[band_row * 32 : band_row * 32 + 16]
            lower = turned[band_row * 32 + 16 : band_row * 32 + 32]
            for half in range(2):
                even, odd = pair_swap(
                    upper[:, half * 128 : half * 128 + 128], lower[:, half * 128 : half * 128 + 128]
                )
                at = view * SEGS + band_row * 4 + half * 2
                blocks_ref[at] = even.astype(BF)
                blocks_ref[at + 1] = odd.astype(BF)


def warp_planes(group, place_ref, order_ref, blocks_ref, interp_ref, first_ref, second_ref, warped_ref):
    first_ref[...] = jnp.zeros_like(first_ref)
    second_ref[...] = jnp.zeros_like(second_ref)

    def step(view, unused):
        for e in range(4):
            plane = order_ref[group * 4 + e]
            base = (view * PLANES + plane) * 64
            rows = []
            for g in range(16):
                taps = [blocks_ref[view * SEGS + place_ref[base + g * 4 + k]] for k in range(4)]
                rows.append(jnp.concatenate(taps, axis=1))
            picked = jnp.concatenate(rows, axis=0)
            matrix = spread_interp(interp_ref[view, plane])
            warped = lax.dot_general(picked, matrix, NN, preferred_element_type=F32)
            first_ref[e] += warped
            second_ref[e] += warped * warped
            warped_ref[view, e] = warped.astype(BF)
        return unused

    lax.fori_loop(0, VIEWS, step, 0, unroll=UNROLL)


def warp_other_kernel(
    place_ref, order_ref, in_ref, interp_ref, blocks_ref, first_ref, second_ref, warped_ref
):
    turn_kernel(in_ref, blocks_ref)
    warp_planes(0, place_ref, order_ref, blocks_ref, interp_ref, first_ref, second_ref, warped_ref)


def warp_mine_kernel(
    place_ref, order_ref, blocks_ref, interp_ref, first_ref, second_ref, warped_ref
):
    warp_planes(1, place_ref, order_ref, blocks_ref, interp_ref, first_ref, second_ref, warped_ref)


UNROLL = 5
SUMS = jax.ShapeDtypeStruct((4, 256, 128), F32)
WARPED = jax.ShapeDtypeStruct((VIEWS, 4, 256, 128), BF)
BLOCKS = jax.ShapeDtypeStruct((VIEWS * SEGS, 16, 128), BF)


def smem():
    return pl.BlockSpec(memory_space=pltpu.SMEM)


def warp_other(place, order, arrived, interp):
    return pl.pallas_call(
        warp_other_kernel,
        in_specs=[smem(), smem(), whole(), whole()],
        out_specs=[whole()] * 4,
        out_shape=[BLOCKS, SUMS, SUMS, WARPED],
        compiler_params=params(),
        name="warp_other",
    )(place, order, arrived, interp)


def warp_mine(place, order, blocks, interp):
    return pl.pallas_call(
        warp_mine_kernel,
        in_specs=[smem(), smem(), whole(), whole()],
        out_specs=[whole()] * 3,
        out_shape=[SUMS, SUMS, WARPED],
        compiler_params=params(),
        name="warp_mine",
    )(place, order, blocks, interp)


CHAINS = 2


def land_views(
    views, place_ref, order_ref, warped_o, warped_m, interp_ref, mean_o, mean_m, grad_ref, out_ref, accs
):
    groups = ((warped_o, mean_o), (warped_m, mean_m))
    for view in views:
        for acc in accs:
            acc[...] = jnp.zeros_like(acc)
        for e in range(8):
            warped_ref, mean_ref = groups[e // 4]
            plane = order_ref[e]
            base = (view * PLANES + plane) * 64
            warped = warped_ref[view, e % 4].astype(F32)
            grad = (grad_ref[plane] * (warped - mean_ref[e % 4].astype(F32))).astype(BF)
            matrix = spread_interp(interp_ref[view, plane])
            spread = lax.dot_general(grad, matrix, NT, preferred_element_type=F32)
            for g in range(16):
                for k in range(4):
                    where = place_ref[base + g * 4 + k]
                    accs[k % 2][where] += spread[g * 16 : (g + 1) * 16, k * 128 : (k + 1) * 128]
        bands = []
        for band_row in range(12):
            columns_up, columns_low = [], []
            for half in range(2):
                at = band_row * 4 + half * 2
                even = accs[0][at] + accs[1][at]
                odd = accs[0][at + 1] + accs[1][at + 1]
                up, low = pair_swap(even, odd)
                columns_up.append(up)
                columns_low.append(low)
            bands.append(jnp.concatenate(columns_up, axis=1))
            bands.append(jnp.concatenate(columns_low, axis=1))
        lane = (view - views[0]) * 384
        out_ref[:, lane : lane + 384] = jnp.concatenate(bands, axis=0).T.astype(BF)


def land_first_kernel(views, *refs):
    land_views(views, *refs[:9], refs[9:])


def land_last_kernel(views, *refs):
    earlier_ref, out_hbm, own_ref, sem = refs[8], refs[9], refs[10], refs[11]
    lanes = earlier_ref.shape[1]
    first = pltpu.make_async_copy(earlier_ref, out_hbm.at[:, 0:lanes], sem.at[0])
    first.start()
    land_views(views, *refs[:8], own_ref, refs[12:])
    last = pltpu.make_async_copy(own_ref, out_hbm.at[:, lanes : VIEWS * 384], sem.at[1])
    last.start()
    first.wait()
    last.wait()


ACCUMULATORS = [pltpu.VMEM((SEGS, 16, 128), F32)] * CHAINS


def land_first(views, *operands):
    return pl.pallas_call(
        functools.partial(land_first_kernel, views),
        in_specs=[smem(), smem()] + [whole()] * 6,
        out_specs=whole(),
        out_shape=jax.ShapeDtypeStruct((256, len(views) * 384), BF),
        scratch_shapes=ACCUMULATORS,
        compiler_params=params(),
        cost_estimate=SMALL,
        name="land_first",
    )(*operands)


def land_last(views, *operands):
    return pl.pallas_call(
        functools.partial(land_last_kernel, views),
        in_specs=[smem(), smem()] + [whole()] * 7,
        out_specs=pl.BlockSpec(memory_space=pltpu.HBM),
        out_shape=pltpu.HBM((256, VIEWS * 384), BF),
        scratch_shapes=[
            pltpu.VMEM((256, len(views) * 384), BF),
            pltpu.SemaphoreType.DMA((2,)),
        ]
        + ACCUMULATORS,
        compiler_params=params(),
        cost_estimate=SMALL,
        name="land_last",
    )(*operands)


def chip_first_kernel(mine_ref, arrived_ref, sum_ref, send_ref):
    total = mine_ref[...] + arrived_ref[...]
    sum_ref[...] = total
    send_ref[...] = total.astype(BF)


def chip_second_kernel(where_ref, mine_ref, arrived_ref, own_ref, send_ref):
    core = where_ref[1]
    own_ref[0:2] = mine_ref[2:4] + arrived_ref[2:4]
    own_ref[2] = mine_ref[core] + arrived_ref[core]
    send_ref[0:2] = mine_ref[0:2] + arrived_ref[0:2]
    send_ref[2] = mine_ref[2 + core] + arrived_ref[2 + core]


def chip_first(mine, arrived):
    return pl.pallas_call(
        chip_first_kernel,
        in_specs=[whole()] * 2,
        out_specs=[whole()] * 2,
        out_shape=[SUMS, jax.ShapeDtypeStruct(SUMS.shape, BF)],
        compiler_params=params(),
        name="chip_first",
    )(mine, arrived)


def chip_second(where, mine, arrived):
    return pl.pallas_call(
        chip_second_kernel,
        in_specs=[smem()] + [whole()] * 2,
        out_specs=[whole()] * 2,
        out_shape=[jax.ShapeDtypeStruct((3, 256, 128), F32)] * 2,
        compiler_params=params(),
        name="chip_second",
    )(where, mine, arrived)


def turned_reference(ref_ref, pair):
    lanes = slice(pair * 128, pair * 128 + 128)
    even, odd = pair_swap(ref_ref[0:16, lanes].astype(F32), ref_ref[16:32, lanes].astype(F32))
    return jnp.concatenate([even, odd], axis=0)


def mean_kernel(sum_ref, there_ref, ref_ref, mean_ref):
    for pair in range(8):
        rows = slice(pair * 32, pair * 32 + 32)
        ref = turned_reference(ref_ref, pair)
        for e in range(4):
            total = sum_ref[e, rows] + there_ref[e ^ 2, rows].astype(F32) + ref
            mean_ref[e, rows] = (total * (1.0 / COUNT)).astype(BF)


def mean_of(sums, there, reference):
    return pl.pallas_call(
        mean_kernel,
        in_specs=[whole()] * 3,
        out_specs=whole(),
        out_shape=jax.ShapeDtypeStruct(SUMS.shape, BF),
        compiler_params=params(),
        name="mean",
    )(sums, there, reference)


def cost_kernel(
    where_ref, first_ref, first_there, second_ref, second_there, ref_ref, low_ref, high_ref, send_ref
):
    y_low, core = where_ref[0], where_ref[1]
    inside = jnp.where(y_low == core, 1.0, 0.0)
    for pair in range(8):
        rows = slice(pair * 32, pair * 32 + 32)
        ref = turned_reference(ref_ref, pair)
        square = ref * ref

        def plane_cost(mine, there, slot):
            first = first_ref[mine, rows] + first_there[there, rows].astype(F32) + ref
            second = second_ref[slot, rows] + second_there[slot, rows] + square
            mean = first * (1.0 / COUNT)
            return second * (1.0 / COUNT) - mean * mean

        low = plane_cost(2, 0, 0)
        high = plane_cost(3, 1, 1)
        far = plane_cost(core, 2 + core, 2)
        low_ref[0, rows] = low.astype(BF)
        high_ref[0, rows] = high.astype(BF)
        send_ref[0, rows] = jnp.where(core == 1, low, high).astype(BF)
        send_ref[1, rows] = (far * inside).astype(BF)


def edges_kernel(where_ref, low_ref, high_ref, near_ref, outer_ref, last_ref, initial_ref):
    core = where_ref[1]
    outer_ref[0] = near_ref[1 - core]
    outer_ref[1] = near_ref[core]
    for local, plane in ((0, outer_ref[0]), (1, low_ref[0]), (2, high_ref[0]), (3, outer_ref[1])):
        last_ref[local] = plane[192:256]
        initial_ref[local] = plane[0:64]


PLANE = jax.ShapeDtypeStruct((1, 256, 128), BF)
PAIR = jax.ShapeDtypeStruct((2, 256, 128), BF)
EDGES = jax.ShapeDtypeStruct((4, 64, 128), BF)


def cost_of(where, first, first_there, second, second_there, reference):
    return pl.pallas_call(
        cost_kernel,
        in_specs=[smem()] + [whole()] * 5,
        out_specs=[whole()] * 3,
        out_shape=[PLANE, PLANE, PAIR],
        compiler_params=params(),
        name="cost",
    )(where, first, first_there, second, second_there, reference)


def edges_of(where, low, high, near):
    return pl.pallas_call(
        edges_kernel,
        in_specs=[smem()] + [whole()] * 3,
        out_specs=[whole()] * 3,
        out_shape=[PAIR, EDGES, EDGES],
        compiler_params=params(),
        name="edges",
    )(where, low, high, near)


def slots_kernel(*refs):
    for slot in range(4):
        refs[4][slot] = refs[slot][...]
        refs[5][slot] = refs[slot][:, :, 768:1024]
        refs[6][slot] = refs[slot][:, :, 0:256]


def slots_of(parts):
    row = jax.ShapeDtypeStruct((4, 2, 8, 256), BF)
    return pl.pallas_call(
        slots_kernel,
        in_specs=[whole()] * 4,
        out_specs=[whole()] * 3,
        out_shape=[jax.ShapeDtypeStruct((4, 2, 8, 1024), BF), row, row],
        compiler_params=params(),
        name="slots",
    )(*parts)


def shifted(values, offset):
    lanes = values.shape[1]
    col = iota(values.shape, 1) & 255
    if offset > 0:
        return jnp.where(col == 255, 0.0, pltpu.roll(values, lanes - 1, 1))
    return jnp.where(col == 0, 0.0, pltpu.roll(values, 1, 1))


def grad_cost_kernel(
    view_ref, own_ref, top_ref, bottom_ref, weight_ref, out_hbm, out_ref, sem
):
    view = view_ref[0]
    padded = []
    for plane in range(PLANES):
        slot = jnp.bitwise_xor(view, plane // 2)
        line = jnp.concatenate(
            [
                top_ref[slot, plane % 2].astype(F32),
                own_ref[slot, plane % 2].astype(F32),
                bottom_ref[slot, plane % 2].astype(F32),
            ],
            axis=1,
        )
        padded.append(jnp.concatenate([shifted(line, 1), line, shifted(line, -1)], axis=0))
    zero = jnp.zeros_like(padded[0])
    weight = weight_ref[...]
    stores = []
    for plane in range(PLANES):
        near = [padded[p] if 0 <= p < PLANES else zero for p in (plane + 1, plane, plane - 1)]
        result = lax.dot_general(
            weight, jnp.concatenate(near, axis=0).astype(BF), NN, preferred_element_type=F32
        )
        grad = result[0:32, 512:1536] + result[32:64, 256:1280] + result[64:96, 0:1024]
        grad = grad * (2.0 / COUNT)
        for pair in range(8):
            upper = grad[0:16, pair * 128 : pair * 128 + 128]
            lower = grad[16:32, pair * 128 : pair * 128 + 128]
            even, odd = pair_swap(upper, lower)
            out_ref[plane, pair * 32 : pair * 32 + 16] = even
            out_ref[plane, pair * 32 + 16 : pair * 32 + 32] = odd
        if plane % 2 == 1:
            part = pl.ds(plane - 1, 2)
            stores.append(
                pltpu.make_async_copy(out_ref.at[part], out_hbm.at[part], sem.at[plane // 2])
            )
            stores[-1].start()
    for store in stores:
        store.wait()


def grad_cost(view, own, top, bottom, weight):
    return pl.pallas_call(
        grad_cost_kernel,
        out_shape=pltpu.HBM((PLANES, 256, 128), F32),
        in_specs=[pl.BlockSpec(memory_space=pltpu.SMEM)] + [whole()] * 4,
        out_specs=pl.BlockSpec(memory_space=pltpu.HBM),
        scratch_shapes=[pltpu.VMEM((PLANES, 256, 128), F32), pltpu.SemaphoreType.DMA((4,))],
        compiler_params=params(),
        name="grad_cost",
    )(view, own, top, bottom, weight)


def line_of(tall, pairs):
    upper, lower = [], []
    for pair in range(pairs):
        up, low = pair_swap(
            tall[pair * 32 : pair * 32 + 16], tall[pair * 32 + 16 : pair * 32 + 32]
        )
        upper.append(up)
        lower.append(low)
    return jnp.concatenate(
        [jnp.concatenate(upper, axis=1), jnp.concatenate(lower, axis=1)], axis=0
    )


def convolved(weight, line):
    wide = jnp.concatenate([shifted(line, -1), line, shifted(line, 1)], axis=0).astype(BF)
    return lax.dot_general(weight, wide, NN, preferred_element_type=F32)


def conv_kernel(outer_ref, low_ref, high_ref, weight_ref, out_ref):
    weight = weight_ref[...]
    results = []
    for plane in (outer_ref[0], low_ref[0], high_ref[0], outer_ref[1]):
        results.append(convolved(weight, line_of(plane.astype(F32), 8)))
    zero = jnp.zeros((8, 256), F32)
    for plane in range(2):
        total = None
        for a in range(3):
            same = results[plane + a][a * 24 + 8 : a * 24 + 16]
            above = results[plane + a][a * 24 : a * 24 + 8, 0:768]
            below = results[plane + a][a * 24 + 16 : a * 24 + 24, 256:1024]
            part = (
                same
                + jnp.concatenate([zero, above], axis=1)
                + jnp.concatenate([below, zero], axis=1)
            )
            total = part if total is None else total + part
        out_ref[plane] = total


def conv_rows_kernel(main_ref, top_ref, bottom_ref, weight_ref, out_ref):
    weight = weight_ref[...]
    results = []
    for local in range(4):
        tall = jnp.concatenate([top_ref[local], bottom_ref[local]], axis=0).astype(F32)
        results.append(convolved(weight, line_of(tall, 4)))
    for plane in range(2):
        first = main_ref[plane, :, 0:256]
        last = main_ref[plane, :, 768:1024]
        for a in range(3):
            first = first + results[plane + a][a * 24 : a * 24 + 8, 0:256]
            last = last + results[plane + a][a * 24 + 16 : a * 24 + 24, 256:512]
        out_ref[plane] = jnp.concatenate(
            [first, main_ref[plane, :, 256:768], last], axis=1
        ).astype(BF)


def conv(outer, low, high, weight):
    return pl.pallas_call(
        conv_kernel,
        out_shape=jax.ShapeDtypeStruct((2, 8, 1024), F32),
        in_specs=[whole()] * 4,
        out_specs=whole(),
        compiler_params=params(),
        name="conv",
    )(outer, low, high, weight)


def conv_rows(main, top, bottom, weight):
    return pl.pallas_call(
        conv_rows_kernel,
        out_shape=jax.ShapeDtypeStruct((2, 8, 1024), BF),
        in_specs=[whole()] * 4,
        out_specs=whole(),
        compiler_params=params(),
        name="conv_rows",
    )(main, top, bottom, weight)


def body(
    source_features,
    reference_features,
    interp,
    source_tile,
    source_block,
    conv_weight,
    grad_regularized,
):
    tiles = lax.axis_size("tile")
    views = lax.axis_size("view")
    view = lax.axis_index("view")
    up = [(i, i + 1) for i in range(tiles - 1)]
    down = [(i + 1, i) for i in range(tiles - 1)]

    def other(array, mask):
        return lax.ppermute(array, "view", [(i, i ^ mask) for i in range(views)])

    slots = jnp.arange(8, dtype=jnp.int32)
    y_low, core = view // 2, view % 2
    order = (
        ((slots // 2) % 2 ^ 1 ^ y_low) * 4 + ((slots // 4) ^ 1 ^ core) * 2 + slots % 2
    ).astype(jnp.int32)
    place = ((source_tile + 1) * 16 + source_block).reshape(-1)

    where = jnp.stack([y_low, core]).astype(jnp.int32)
    own = grad_regularized
    parts = (own, other(own, 1), other(own, 2), other(own, 3))
    operand = strips(source_features.reshape(1280, 128))
    cotangent, last, initial = slots_of(parts)
    operand, last, initial = lax.optimization_barrier((operand, last, initial))
    arrived = lax.all_to_all(operand, "tile", split_axis=0, concat_axis=0, tiled=True)
    top = lax.ppermute(last, "tile", up)
    bottom = lax.ppermute(initial, "tile", down)
    back_weight = conv_weight.transpose(1, 4, 0, 2, 3).reshape(96, 72)
    weight = conv_weight.transpose(0, 1, 3, 2, 4).reshape(72, 96)
    grad = grad_cost(view.astype(jnp.int32).reshape(1), cotangent, top, bottom, back_weight)
    arrived, grad, weight = lax.optimization_barrier((arrived, grad, weight))

    blocks, first_o, second_o, warped_o = warp_other(place, order, arrived, interp)
    first_m, second_m, warped_m = warp_mine(place, order, blocks, interp)
    first_chip, first_send = chip_first(first_m, other(first_o, 1))
    first_there = other(first_send, 2)
    second_own, second_send = chip_second(where, second_m, other(second_o, 1))
    second_there = other(second_send, 2)
    first_there, second_own = lax.optimization_barrier((first_there, second_own))
    mean_mine = mean_of(first_chip, first_there, reference_features)
    mean_other = other(mean_mine, 1)

    shared = (place, order, warped_o, warped_m, interp, mean_other, mean_mine, grad)
    landed = land_first((0, 1, 2, 3), *shared)
    landed, second_there = lax.optimization_barrier((landed, second_there))
    low, high, send = cost_of(
        where, first_chip, first_there, second_own, second_there, reference_features
    )
    near = other(send, 1)
    landed = land_last((4,), *shared, landed)
    landed, near = lax.optimization_barrier((landed, near))
    outer, cost_last, cost_initial = edges_of(where, low, high, near)
    landed, cost_last, cost_initial = lax.optimization_barrier((landed, cost_last, cost_initial))
    returned = lax.all_to_all(landed, "tile", split_axis=0, concat_axis=0, tiled=True)
    cost_top = lax.ppermute(cost_last, "tile", up)
    cost_bottom = lax.ppermute(cost_initial, "tile", down)
    regularized = conv_rows(conv(outer, low, high, weight), cost_top, cost_bottom, weight)

    grad_source = unstrips(returned).reshape(source_features.shape)
    return regularized, grad_source


def solution(mesh):
    return jax.shard_map(
        body,
        mesh=mesh,
        in_specs=(
            P("view", None, "tile", None),
            P(None, "tile"),
            P("view", None, None, None, None),
            P("view", None, "tile", None),
            P("view", None, "tile", None),
            P(),
            P("view", None, "tile"),
        ),
        out_specs=(P("view", None, "tile"), P("view", None, "tile", None)),
        check_vma=False,
    )
```
